512 devices in a mesh: section: 32 (over z, x_hi, core), tensor: 16 (over x_lo, y).
Axes of the slice: x: 4 (x_hi: 2, x_lo: 2; x = x_hi * 2 + x_lo), y: 8, z: 8, core: 2. Of those that a mesh axis runs over, the one named last changes fastest.
Arguments:
- held: bfloat16 [32, 2, 256, 12288], P('section', None, None, 'tensor'), may hold values from -6 to 6
- norm_gain: float32 [32, 2, 12288], P('section', None, 'tensor'), may hold values from 0.1 to 1.9
- key_gain: float32 [32, 2, 12288], P('section', None, 'tensor'), may hold values from -2 to 2
- evict_slot: int32 [32], P('section'), may hold values from 0 to 1
- evict_step: int32 [32], P('section'), may hold values from 0 to 1
Outputs:
- final: bfloat16 [32, 2, 256, 12288], P('section', None, None, 'tensor')
- mirror_store: bfloat16 [32, 256, 12288], P('section', None, 'tensor')
The draws below stay inside these ranges and needn't reach their ends.
All inputs are finite; a program needn't handle non-finite values.
Results may differ from the reference program's by a relative error of at most 0.039.
Values may be sent and summed in bfloat16 or wider, within the bound.
No kernel may reach another device: no remote copies, remote signals or barrier semaphores. Data moves between devices by JAX's collectives and lax.ppermute only.
A program may use at most 64 MiB of HBM per device.

```python
import jax
import jax.numpy as jnp
from jax import lax

D = 12288
HEAD = 128
LEN = 256
MB = 2
LAYERS = 2
STEPS = 2
N_SECTION = 32


def set_ends(result, stream_key, smallest, largest):
    shape = result.shape
    place = [jax.random.randint(jax.random.fold_in(stream_key, axis), (), 0, shape[axis]) for axis in range(len(shape))]
    result = result.at[tuple(place)].set(smallest)
    longest = shape.index(max(shape))
    place[longest] = (place[longest] + 1) % shape[longest]
    return result.at[tuple(place)].set(largest)


def levels(stream_key, dims, cuts, low, high):
    factor_of, own = 1.0, jax.random.fold_in(stream_key, 6)
    for axis_at, shards_of in cuts:
        heights = jnp.exp(jax.random.uniform(jax.random.fold_in(own, axis_at), (shards_of,), jnp.float32, low / len(cuts), high / len(cuts)))
        factor_of = factor_of * jnp.repeat(heights, dims[axis_at] // shards_of).reshape([-1 if axis == axis_at else 1 for axis in range(len(dims))])
    return factor_of


def bell_draw(own_key, dims, scale, limit, pieces=(), held_as=jnp.bfloat16):
    drawn = jax.random.normal(own_key, dims, jnp.float32) * scale
    if len(pieces) > 0:
        drawn = levels(own_key, dims, pieces, -0.22, 0.18) * drawn
    return jnp.clip(drawn, min=-limit, max=limit).astype(held_as)


def setup_inputs(seed: int = 0) -> dict:
    arg_keys = jax.random.split(jax.random.key(seed), 6)
    held = bell_draw(arg_keys[0], (N_SECTION, MB, LEN, D), 1.0, 6.0, ((0, 32), (3, 16)))
    norm_gain = jnp.clip(1.0 + 0.18 * jax.random.normal(arg_keys[1], (N_SECTION, LAYERS, D), jnp.float32), 0.1, 1.9)
    key_gain = jnp.clip(jax.random.uniform(arg_keys[2], (N_SECTION, LAYERS, D), jnp.float32, -2.0, 2.0) * levels(arg_keys[2], (N_SECTION, LAYERS, D), ((0, 32), (2, 16)), -0.4, 0.0), -2.0, 2.0)
    evict_slot = set_ends(jax.random.randint(arg_keys[3], (N_SECTION,), 0, MB), jax.random.fold_in(arg_keys[3], 1), 0, MB - 1).astype(jnp.int32)
    evict_step = set_ends(jax.random.randint(arg_keys[4], (N_SECTION,), 0, STEPS), jax.random.fold_in(arg_keys[4], 1), 0, STEPS - 1).astype(jnp.int32)
    return {"held": held, "norm_gain": norm_gain, "key_gain": key_gain, "evict_slot": evict_slot, "evict_step": evict_step}


def attention_layer(act, ngain, kgain):
    xf = act.astype(jnp.float32)
    ms = lax.optimization_barrier(jnp.mean(xf * xf, axis=-1, keepdims=True))
    h = xf * lax.rsqrt(ms + 1e-05) * ngain
    query = h.astype(jnp.bfloat16)
    keys = (h * kgain).astype(jnp.bfloat16)
    batch, length, width = act.shape
    heads = width // HEAD
    qh = query.reshape(batch, length, heads, HEAD).astype(jnp.float32)
    kh = keys.reshape(batch, length, heads, HEAD).astype(jnp.float32)
    scores = jnp.einsum('bqhd,bkhd->bhqk', qh, kh) / jnp.sqrt(jnp.float32(HEAD))
    rows = lax.broadcasted_iota(jnp.int32, (length, length), 0)
    cols = lax.broadcasted_iota(jnp.int32, (length, length), 1)
    scores = jnp.where(cols <= rows, scores, jnp.float32(-1e+30))
    top = lax.optimization_barrier(jnp.max(scores, axis=-1, keepdims=True))
    expo = jnp.exp(scores - top)
    probs = (expo / lax.optimization_barrier(jnp.sum(expo, axis=-1, keepdims=True))).astype(jnp.bfloat16)
    out = jnp.einsum('bhqk,bkhd->bqhd', probs.astype(jnp.float32), qh)
    return (xf + out.reshape(batch, length, width)).astype(jnp.bfloat16)

def section_layers(args):
    act, ngain, kgain = args
    for layer in range(LAYERS):
        act = attention_layer(act, ngain[layer], kgain[layer])
    return act

def reference(held, norm_gain, key_gain, evict_slot, evict_step):
    acts = held
    captured = jnp.zeros((N_SECTION, LEN, D), jnp.bfloat16)
    sections = jnp.arange(N_SECTION, dtype=jnp.int32)
    for step in range(STEPS):
        fresh = lax.map(section_layers, (acts, norm_gain, key_gain))
        picked = fresh[sections, evict_slot]
        captured = jnp.where((evict_step == step)[:, None, None], picked, captured)
        acts = jnp.roll(fresh, 1, axis=0)
    return (acts, captured[::-1])
```

```python
import functools

import jax
import jax.numpy as jnp
from jax import lax
from jax.experimental import pallas as pl
from jax.experimental.pallas import tpu as pltpu
from jax.sharding import PartitionSpec as P

D = 12288
HEAD = 128
LAYERS = 2
STEPS = 2
BLOCK = 128
EPS = 1e-5
SCORE = 1.4426950408889634 / HEAD**0.5


def one_micro_batch(x_ref, total, ngain, kgain, y_ref, b):
    length, width = x_ref.shape[1:]
    blocks = length // BLOCK
    inv = lax.rsqrt(total / D + EPS)
    scale = jnp.concatenate(
        [jnp.broadcast_to(inv[i : i + 1, :], (BLOCK, BLOCK)).T for i in range(blocks)], axis=0
    )
    rows = lax.broadcasted_iota(jnp.int32, (BLOCK, BLOCK), 0)
    cols = lax.broadcasted_iota(jnp.int32, (BLOCK, BLOCK), 1)
    keep = cols <= rows
    ones = jnp.ones((length, HEAD), jnp.bfloat16)
    squares = [jnp.zeros((BLOCK, HEAD), jnp.float32) for _ in range(blocks)]
    for head in range(width // HEAD):
        at = slice(head * HEAD, (head + 1) * HEAD)
        xf = x_ref[b, :, at].astype(jnp.float32)
        h = xf * scale * ngain[:, at]
        query = h.astype(jnp.bfloat16)
        keys = (h * (kgain[:, at] * SCORE)).astype(jnp.bfloat16)
        values = jnp.concatenate([query, ones], axis=1)
        for i in range(blocks):
            here = slice(i * BLOCK, (i + 1) * BLOCK)
            seen = (i + 1) * BLOCK
            s = lax.dot_general(
                query[here], keys[:seen], (((1,), (1,)), ((), ())), preferred_element_type=jnp.float32
            )
            last = jnp.where(keep, s[:, i * BLOCK :], jnp.float32(-1e30))
            s = last if i == 0 else jnp.concatenate([s[:, : i * BLOCK], last], axis=1)
            p = jnp.exp2(s - jnp.max(s, axis=1, keepdims=True)).astype(jnp.bfloat16)
            o = jnp.dot(p, values[:seen], preferred_element_type=jnp.float32)
            y = (xf[here] + o[:, :HEAD] / o[:, HEAD:]).astype(jnp.bfloat16)
            y_ref[b, here, at] = y
            yf = y.astype(jnp.float32)
            squares[i] = squares[i] + yf * yf
    return [jnp.sum(sq.T, axis=0, keepdims=True) for sq in squares]


def layer_kernel(x_ref, parts_ref, ngain_ref, kgain_ref, y_ref, squares_ref):
    batch, length, _ = x_ref.shape
    blocks = length // BLOCK
    totals = jnp.sum(parts_ref[...], axis=0)
    found = []
    for b in range(batch):
        found += one_micro_batch(
            x_ref, totals[b * blocks : (b + 1) * blocks], ngain_ref[...], kgain_ref[...], y_ref, b
        )
    rows = jnp.concatenate(found, axis=0)
    squares_ref[...] = jnp.broadcast_to(rows[None], squares_ref.shape)


def layer(x, parts, ngain, kgain):
    vmem = pl.BlockSpec(memory_space=pltpu.VMEM)
    return pl.pallas_call(
        layer_kernel,
        out_shape=(jax.ShapeDtypeStruct(x.shape, x.dtype), jax.ShapeDtypeStruct(parts.shape, parts.dtype)),
        in_specs=[vmem] * 4,
        out_specs=(vmem, vmem),
        compiler_params=pltpu.CompilerParams(vmem_limit_bytes=32 * 1024 * 1024),
        cost_estimate=pl.CostEstimate(flops=400_000_000, bytes_accessed=2_000_000, transcendentals=800_000),
        name="layer",
    )(x, parts, ngain, kgain)


def squares_kernel(x_ref, squares_ref):
    batch, length, width = x_ref.shape
    found = []
    for b in range(batch):
        for i in range(length // BLOCK):
            sq = jnp.zeros((BLOCK, HEAD), jnp.float32)
            for head in range(width // HEAD):
                xf = x_ref[b, i * BLOCK : (i + 1) * BLOCK, head * HEAD : (head + 1) * HEAD].astype(jnp.float32)
                sq = sq + xf * xf
            found.append(jnp.sum(sq.T, axis=0, keepdims=True))
    squares_ref[...] = jnp.broadcast_to(jnp.concatenate(found, axis=0)[None], squares_ref.shape)


def first_squares(x, members):
    batch, length, _ = x.shape
    vmem = pl.BlockSpec(memory_space=pltpu.VMEM)
    return pl.pallas_call(
        squares_kernel,
        out_shape=jax.ShapeDtypeStruct((members, batch * length // BLOCK, BLOCK), jnp.float32),
        in_specs=[vmem],
        out_specs=vmem,
        compiler_params=pltpu.CompilerParams(vmem_limit_bytes=32 * 1024 * 1024),
        name="squares",
    )(x)


def exchange(parts, groups):
    return lax.all_to_all(parts, "tensor", 0, 0, axis_index_groups=groups, tiled=True)


def near_and_far():
    half = lax.axis_size("tensor") // 2
    near = [[x * half + y + i for x in range(2) for i in range(2)] for y in range(0, half, 2)]
    far = [[x * half + y for y in range(i, half, 2)] for x in range(2) for i in range(2)]
    return near, far


def gather_sums(parts):
    near, far = near_and_far()
    part = jnp.sum(exchange(parts, near), axis=0)
    return exchange(jnp.broadcast_to(part[None], parts.shape), far)


def send(value, target):
    count = lax.axis_size("section")
    return lax.ppermute(value, "section", [(s, target(s) % count) for s in range(count)])


def shards(held, norm_gain, key_gain, evict_slot, evict_step):
    act = held[0]
    count = lax.axis_size("section")
    facts = jnp.concatenate([evict_slot, evict_step]).astype(jnp.float32)
    facts = jnp.broadcast_to(facts[None, :, None], (1, 2, norm_gain.shape[2]))
    ours = jnp.concatenate([norm_gain, key_gain, facts], axis=1)
    theirs = send(ours, lambda s: s - 1)
    slot_next = theirs[0, 2 * LAYERS, 0].astype(jnp.int32)
    parts = first_squares(act, 4)
    kept = None
    for step, gains in enumerate((ours, theirs)):
        for at in range(LAYERS):
            act, parts = layer(act, gather_sums(parts), gains[:, at], gains[:, LAYERS + at])
        if step == 0:
            kept = lax.dynamic_index_in_dim(act, evict_slot[0], 0, keepdims=False)
    late = send(lax.dynamic_index_in_dim(act, slot_next, 0, keepdims=False), lambda s: s + 1)
    captured = jnp.where(evict_step[0] == 0, kept, late)
    stored = send(captured, lambda s: count - 1 - s)
    final = send(act, lambda s: s + STEPS)
    return (final[None], stored[None])


def solution(mesh):
    return jax.shard_map(
        shards,
        mesh=mesh,
        in_specs=(
            P("section", None, None, "tensor"),
            P("section", None, "tensor"),
            P("section", None, "tensor"),
            P("section"),
            P("section"),
        ),
        out_specs=(P("section", None, None, "tensor"), P("section", None, "tensor")),
        check_vma=False,
    )
```

```python
import functools

import jax
import jax.numpy as jnp
from jax import lax
from jax.experimental import pallas as pl
from jax.experimental.pallas import tpu as pltpu
from jax.sharding import PartitionSpec as P

D = 12288
HEAD = 128
LAYERS = 2
BLOCK = 128
EPS = 1e-5
SCORE = 1.4426950408889634 / HEAD**0.5
X_LO = X_HI = CORES = 2

VMEM = pl.BlockSpec(memory_space=pltpu.VMEM)
PARAMS = pltpu.CompilerParams(vmem_limit_bytes=32 * 1024 * 1024)


def call(kernel, out_shape, name, mflop=1):
    several = isinstance(out_shape, tuple)

    def run(*operands):
        return pl.pallas_call(
            kernel,
            out_shape=out_shape,
            in_specs=[VMEM] * len(operands),
            out_specs=(VMEM,) * len(out_shape) if several else VMEM,
            compiler_params=PARAMS,
            cost_estimate=pl.CostEstimate(
                flops=mflop * 1_000_000, bytes_accessed=1_000_000, transcendentals=mflop * 2_000
            ),
            name=name,
        )(*operands)

    return run


def f32(*shape):
    return jax.ShapeDtypeStruct(shape, jnp.float32)


def bf16(*shape):
    return jax.ShapeDtypeStruct(shape, jnp.bfloat16)


def column(total):
    inv = lax.rsqrt(total / D + EPS)
    rows = [jnp.broadcast_to(inv[i : i + 1], (BLOCK, BLOCK)).T for i in range(inv.shape[0])]
    return jnp.concatenate(rows, axis=0)


def head_layer(xf, scale, ngain, kgain):
    length = xf.shape[0]
    keep = lax.broadcasted_iota(jnp.int32, (BLOCK, BLOCK), 1) <= lax.broadcasted_iota(jnp.int32, (BLOCK, BLOCK), 0)
    h = xf * scale * ngain
    query = h.astype(jnp.bfloat16)
    keys = (h * (kgain * SCORE)).astype(jnp.bfloat16)
    values = jnp.concatenate([query, jnp.ones((length, HEAD), jnp.bfloat16)], axis=1)
    out = []
    for i in range(length // BLOCK):
        here = slice(i * BLOCK, (i + 1) * BLOCK)
        seen = (i + 1) * BLOCK
        s = lax.dot_general(
            query[here], keys[:seen], (((1,), (1,)), ((), ())), preferred_element_type=jnp.float32
        )
        last = jnp.where(keep, s[:, i * BLOCK :], jnp.float32(-1e30))
        s = last if i == 0 else jnp.concatenate([s[:, : i * BLOCK], last], axis=1)
        p = jnp.exp2(s - jnp.max(s, axis=1, keepdims=True)).astype(jnp.bfloat16)
        o = jnp.dot(p, values[:seen], preferred_element_type=jnp.float32)
        out.append((xf[here] + o[:, :HEAD] / o[:, HEAD:]).astype(jnp.bfloat16))
    return jnp.concatenate(out, axis=0)


def token_sums(squares, out_ref):
    rows = []
    for sq in squares:
        for i in range(sq.shape[0] // BLOCK):
            rows.append(jnp.sum(sq[i * BLOCK : (i + 1) * BLOCK].T, axis=0, keepdims=True))
    out_ref[...] = jnp.broadcast_to(jnp.concatenate(rows, axis=0)[None], out_ref.shape)


def lanes(head):
    return slice(head * HEAD, (head + 1) * HEAD)


class Pack:
    def __init__(self, heads, batch, blocks):
        self.heads, self.rows = heads, batch * blocks
        self.gains = 2 * LAYERS * heads
        self.slot = self.gains + LAYERS * self.rows
        self.step = self.slot + 1
        self.size = -(-(self.step + 1) // 8) * 8

    def ngain(self, ref, layer, head):
        at = layer * self.heads + head
        return ref[at : at + 1, :]

    def kgain(self, ref, layer, head):
        return self.ngain(ref, LAYERS + layer, head)

    def sums(self, ref, layer):
        at = self.gains + layer * self.rows
        return ref[at : at + self.rows, :]


def first_kernel(x_ref, out_ref):
    batch, _, width = x_ref.shape
    found = []
    for b in range(batch):
        sq = 0.0
        for head in range(width // HEAD):
            xf = x_ref[b, :, lanes(head)].astype(jnp.float32)
            sq = sq + xf * xf
        found.append(sq)
    token_sums(found, out_ref)


def layer_kernel(pack, layer, with_y, with_sums, x_ref, parts_ref, pack_ref, *outs):
    batch, length, width = x_ref.shape
    y_ref = outs[0] if with_y else None
    blocks = length // BLOCK
    totals = jnp.sum(parts_ref[...], axis=0)
    found = []
    for b in range(batch):
        scale = column(totals[b * blocks : (b + 1) * blocks])
        sq = 0.0
        for head in range(width // HEAD):
            xf = x_ref[b, :, lanes(head)].astype(jnp.float32)
            y = head_layer(xf, scale, pack.ngain(pack_ref, layer, head), pack.kgain(pack_ref, layer, head))
            if with_y:
                y_ref[b, :, lanes(head)] = y
            if with_sums:
                yf = y.astype(jnp.float32)
                sq = sq + yf * yf
        found.append(sq)
    if with_sums:
        token_sums(found, outs[-1])


def pack_kernel(pack, parts0_ref, parts1_ref, head_ref, out_ref):
    out_ref[...] = head_ref[...]
    for layer, ref in enumerate((parts0_ref, parts1_ref)):
        at = pack.gains + layer * pack.rows
        out_ref[at : at + pack.rows, :] = jnp.sum(ref[...], axis=0)


def repeat_kernel(pack, *refs):
    *x_refs, pack_ref, y_ref, out_ref = refs
    blocks = x_refs[0].shape[0] // BLOCK
    found = []
    for b, x_ref in enumerate(x_refs):
        scales = [column(pack.sums(pack_ref, at)[b * blocks : (b + 1) * blocks]) for at in range(LAYERS)]
        sq = 0.0
        for head in range(pack.heads):
            yf = x_ref[:, lanes(head)].astype(jnp.float32)
            for at in range(LAYERS):
                y = head_layer(yf, scales[at], pack.ngain(pack_ref, at, head), pack.kgain(pack_ref, at, head))
                yf = y.astype(jnp.float32)
            y_ref[b, :, lanes(head)] = y
            sq = sq + yf * yf
        found.append(sq)
    token_sums(found, out_ref)


def keep_kernel(pack, x_ref, carry_ref, own_ref, behind_ref, v_ref):
    length = x_ref.shape[1]
    blocks = length // BLOCK
    second = own_ref[pack.slot : pack.slot + 1, :] > 0.5
    late = own_ref[pack.step : pack.step + 1, :] > 0.5
    scales = []
    for at in range(LAYERS):
        total = jnp.where(late, pack.sums(behind_ref, at), pack.sums(own_ref, at))
        scales.append(column(jnp.where(second, total[blocks : 2 * blocks], total[:blocks])))
    for head in range(pack.heads):
        own = jnp.where(second, x_ref[1, :, lanes(head)].astype(jnp.float32), x_ref[0, :, lanes(head)].astype(jnp.float32))
        yf = jnp.where(late, carry_ref[:, lanes(head)].astype(jnp.float32), own)
        for at in range(LAYERS):
            ngain = jnp.where(late, pack.ngain(behind_ref, at, head), pack.ngain(own_ref, at, head))
            kgain = jnp.where(late, pack.kgain(behind_ref, at, head), pack.kgain(own_ref, at, head))
            y = head_layer(yf, scales[at], ngain, kgain)
            yf = y.astype(jnp.float32)
        v_ref[:, lanes(head)] = y


def store_kernel(pack, v_ref, pack_ref, out_ref):
    blocks = v_ref.shape[0] // BLOCK
    second = pack_ref[pack.slot : pack.slot + 1, :] > 0.5
    late = pack_ref[pack.step : pack.step + 1, :] > 0.5
    scales = []
    for at in range(LAYERS):
        total = pack.sums(pack_ref, at)
        scales.append(column(jnp.where(second, total[blocks : 2 * blocks], total[:blocks])))
    for head in range(pack.heads):
        start = v_ref[:, lanes(head)].astype(jnp.float32)
        yf = start
        for at in range(LAYERS):
            y = head_layer(yf, scales[at], pack.ngain(pack_ref, at, head), pack.kgain(pack_ref, at, head))
            yf = y.astype(jnp.float32)
        out_ref[:, lanes(head)] = jnp.where(late, yf, start).astype(jnp.bfloat16)


def exchange(parts):
    return lax.all_to_all(parts, "tensor", 0, 0, tiled=True)


def send(value, target):
    count = lax.axis_size("section")
    return lax.ppermute(value, "section", [(s, target(s) % count) for s in range(count)])


def back_around_x(value):
    sections, members = lax.axis_size("section"), lax.axis_size("tensor")
    ys = members // X_LO
    layers_z = sections // (X_HI * CORES)
    first, second = [], []
    for z in range(layers_z):
        for x in range(X_HI * X_LO):
            for core in range(CORES):
                for y in range(ys):

                    def flat(z, x):
                        section = ((z % layers_z) * X_HI + x // X_LO) * CORES + core
                        return section * members + (x % X_LO) * ys + y

                    count = X_HI * X_LO
                    middle, last = (x - 1) % count, (x - 2) % count
                    first.append((flat(z, x), flat(z, middle)))
                    second.append((flat(z, middle), flat(z + x // X_LO, last)))
    axes = ("section", "tensor")
    return lax.ppermute(lax.ppermute(value, axes, first), axes, second)


def shards(held, norm_gain, key_gain, evict_slot, evict_step):
    x = held[0]
    batch, length, width = x.shape
    heads = width // HEAD
    pack = Pack(heads, batch, length // BLOCK)
    sections, members = lax.axis_size("section"), lax.axis_size("tensor")
    sums = f32(members, pack.rows, BLOCK)
    facts = jnp.concatenate([evict_slot, evict_step]).astype(jnp.float32)
    facts = jnp.broadcast_to(facts[:, None], (2, HEAD))
    empty = jnp.zeros((pack.size, HEAD), jnp.float32)
    head = jnp.concatenate(
        [
            norm_gain.reshape(-1, HEAD),
            key_gain.reshape(-1, HEAD),
            empty[pack.gains : pack.slot],
            facts,
            empty[pack.step + 1 :],
        ],
        axis=0,
    )

    first_ahead = send(x[0], lambda s: s + 2)
    second_ahead = back_around_x(x[1])
    slot_next = send(evict_slot, lambda s: s - 1)[0]
    carry = send(lax.dynamic_index_in_dim(x, slot_next, 0, keepdims=False), lambda s: s + 1)

    parts1 = exchange(call(first_kernel, sums, "first_sums")(x))
    layer1 = functools.partial(layer_kernel, pack, 0, False, True)
    parts2 = exchange(call(layer1, sums, "home_layer", 400)(x, parts1, head))
    own = call(functools.partial(pack_kernel, pack), f32(pack.size, HEAD), "own_pack")(parts1, parts2, head)
    behind = send(own, lambda s: s + 1)
    behind2 = send(own, lambda s: s + 2)

    repeat = call(functools.partial(repeat_kernel, pack), (bf16(*x.shape), sums), "repeat", 800)
    y, found = repeat(first_ahead, second_ahead, behind2)
    parts3 = exchange(found)
    kept = call(functools.partial(keep_kernel, pack), bf16(length, width), "keep", 400)(x, carry, own, behind)
    kept = send(kept, lambda s: sections - 1 - s)
    layer3 = functools.partial(layer_kernel, pack, 0, True, True)
    y, found = call(layer3, (bf16(*x.shape), sums), "third_layer", 400)(y, parts3, behind)
    parts4 = exchange(found)
    late = call(functools.partial(pack_kernel, pack), f32(pack.size, HEAD), "late_pack")(parts3, parts4, behind)
    late = send(late, lambda s: -s)
    layer4 = functools.partial(layer_kernel, pack, 1, True, False)
    (final,) = call(layer4, (bf16(*x.shape),), "fourth_layer", 400)(y, parts4, behind)
    stored = call(functools.partial(store_kernel, pack), bf16(length, width), "store", 400)(kept, late)
    return (final[None], stored[None])


def solution(mesh):
    return jax.shard_map(
        shards,
        mesh=mesh,
        in_specs=(
            P("section", None, None, "tensor"),
            P("section", None, "tensor"),
            P("section", None, "tensor"),
            P("section"),
            P("section"),
        ),
        out_specs=(P("section", None, None, "tensor"), P("section", None, "tensor")),
        check_vma=False,
    )
```

```python
import functools

import jax
import jax.numpy as jnp
from jax import lax
from jax.experimental import pallas as pl
from jax.experimental.pallas import tpu as pltpu
from jax.sharding import PartitionSpec as P

D = 12288
HEAD = 128
LAYERS = 2
BLOCK = 128
EPS = 1e-5
SCORE = 1.4426950408889634 / HEAD**0.5
X_LO = X_HI = CORES = 2

VMEM = pl.BlockSpec(memory_space=pltpu.VMEM)
PARAMS = pltpu.CompilerParams(vmem_limit_bytes=32 * 1024 * 1024)


def call(kernel, out_shape, name, mflop=1):
    several = isinstance(out_shape, tuple)

    def run(*operands):
        return pl.pallas_call(
            kernel,
            out_shape=out_shape,
            in_specs=[VMEM] * len(operands),
            out_specs=(VMEM,) * len(out_shape) if several else VMEM,
            compiler_params=PARAMS,
            cost_estimate=pl.CostEstimate(
                flops=mflop * 1_000_000, bytes_accessed=1_000_000, transcendentals=mflop * 2_000
            ),
            name=name,
        )(*operands)

    return run


def f32(*shape):
    return jax.ShapeDtypeStruct(shape, jnp.float32)


def bf16(*shape):
    return jax.ShapeDtypeStruct(shape, jnp.bfloat16)


def column(total):
    inv = lax.rsqrt(total / D + EPS)
    rows = [jnp.broadcast_to(inv[i : i + 1], (BLOCK, BLOCK)).T for i in range(inv.shape[0])]
    return jnp.concatenate(rows, axis=0)


def head_layer(xf, scale, ngain, kgain):
    length = xf.shape[0]
    keep = lax.broadcasted_iota(jnp.int32, (BLOCK, BLOCK), 1) <= lax.broadcasted_iota(jnp.int32, (BLOCK, BLOCK), 0)
    h = xf * scale * ngain
    query = h.astype(jnp.bfloat16)
    keys = (h * (kgain * SCORE)).astype(jnp.bfloat16)
    values = jnp.concatenate([query, jnp.ones((length, HEAD), jnp.bfloat16)], axis=1)
    out = []
    for i in range(length // BLOCK):
        here = slice(i * BLOCK, (i + 1) * BLOCK)
        seen = (i + 1) * BLOCK
        s = lax.dot_general(
            query[here], keys[:seen], (((1,), (1,)), ((), ())), preferred_element_type=jnp.float32
        )
        last = jnp.where(keep, s[:, i * BLOCK :], jnp.float32(-1e30))
        s = last if i == 0 else jnp.concatenate([s[:, : i * BLOCK], last], axis=1)
        p = jnp.exp2(s - jnp.max(s, axis=1, keepdims=True)).astype(jnp.bfloat16)
        o = jnp.dot(p, values[:seen], preferred_element_type=jnp.float32)
        out.append((xf[here] + o[:, :HEAD] / o[:, HEAD:]).astype(jnp.bfloat16))
    return jnp.concatenate(out, axis=0)


def token_sums(squares, out_ref):
    rows = []
    for sq in squares:
        for i in range(sq.shape[0] // BLOCK):
            rows.append(jnp.sum(sq[i * BLOCK : (i + 1) * BLOCK].T, axis=0, keepdims=True))
    out_ref[...] = jnp.broadcast_to(jnp.concatenate(rows, axis=0)[None], out_ref.shape)


def lanes(head):
    return slice(head * HEAD, (head + 1) * HEAD)


class Pack:
    def __init__(self, heads, batch, blocks):
        self.heads, self.rows = heads, batch * blocks
        self.sums = slice(2 * LAYERS * heads, 2 * LAYERS * heads + self.rows)
        self.slot = self.sums.stop
        self.step = self.slot + 1
        self.size = -(-(self.step + 1) // 8) * 8

    def gains(self, ref, layer, head):
        at = [(part * LAYERS + layer) * self.heads + head for part in range(2)]
        return [ref[i : i + 1, :] for i in at]

    def second(self, ref):
        return ref[self.slot : self.slot + 1, :] > 0.5

    def late(self, ref):
        return ref[self.step : self.step + 1, :] > 0.5


def first_kernel(x_ref, out_ref):
    batch, _, width = x_ref.shape
    found = []
    for b in range(batch):
        sq = 0.0
        for head in range(width // HEAD):
            xf = x_ref[b, :, lanes(head)].astype(jnp.float32)
            sq = sq + xf * xf
        found.append(sq)
    token_sums(found, out_ref)


def layer_kernel(pack, layer, split, outputs, *refs):
    x_refs = refs[:2] if split else [refs[0].at[b] for b in range(refs[0].shape[0])]
    refs = list(refs[2 if split else 1 :])
    parts_ref = refs.pop(0) if "parts" in outputs else None
    pack_ref = refs.pop(0)
    y_ref = refs.pop(0) if "y" in outputs else None
    pick_ref = refs.pop(0) if "pick" in outputs else None
    sums_ref = refs.pop(0) if "sums" in outputs else None
    blocks = x_refs[0].shape[0] // BLOCK
    totals = pack_ref[pack.sums, :] if parts_ref is None else jnp.sum(parts_ref[...], axis=0)
    found = []
    for b, x_ref in enumerate(x_refs):
        scale = column(totals[b * blocks : (b + 1) * blocks])
        sq = 0.0
        for head in range(pack.heads):
            xf = x_ref[:, lanes(head)].astype(jnp.float32)
            y = head_layer(xf, scale, *pack.gains(pack_ref, layer, head))
            if y_ref is not None:
                y_ref[b, :, lanes(head)] = y
            if sums_ref is not None:
                yf = y.astype(jnp.float32)
                sq = sq + yf * yf
        found.append(sq)
    if pick_ref is not None:
        second = pack.second(pack_ref)
        for head in range(pack.heads):
            pick_ref[:, lanes(head)] = either(second, y_ref[1, :, lanes(head)], y_ref[0, :, lanes(head)])
    if sums_ref is not None:
        token_sums(found, sums_ref)


def either(condition, there, here):
    return jnp.where(condition, there.astype(jnp.float32), here.astype(jnp.float32)).astype(jnp.bfloat16)


def pack_kernel(pack, parts_ref, rest_ref, out_ref):
    out_ref[...] = rest_ref[...]
    out_ref[pack.sums, :] = jnp.sum(parts_ref[...], axis=0)


def choose_kernel(pack, y_ref, carry_ref, pack_ref, out_ref):
    second, late = pack.second(pack_ref), pack.late(pack_ref)
    for head in range(pack.heads):
        at = lanes(head)
        out_ref[:, at] = either(late, either(second, y_ref[1, :, at], y_ref[0, :, at]), carry_ref[:, at])


def mirror_kernel(pack, layer, x_ref, *refs):
    *parts_ref, pack_ref, out_ref = refs
    kept_ref = parts_ref.pop(0) if layer else x_ref
    blocks = x_ref.shape[0] // BLOCK
    totals = jnp.sum(parts_ref[0][...], axis=0) if parts_ref else pack_ref[pack.sums, :]
    scale = column(jnp.where(pack.second(pack_ref), totals[blocks : 2 * blocks], totals[:blocks]))
    late = pack.late(pack_ref)
    for head in range(pack.heads):
        xf = x_ref[:, lanes(head)].astype(jnp.float32)
        y = head_layer(xf, scale, *pack.gains(pack_ref, layer, head))
        out_ref[:, lanes(head)] = either(late, y, kept_ref[:, lanes(head)])


def exchange(parts):
    return lax.all_to_all(parts, "tensor", 0, 0, tiled=True)


def send(value, target):
    count = lax.axis_size("section")
    return lax.ppermute(value, "section", [(s, target(s) % count) for s in range(count)])


def around_x(hop):
    sections, members = lax.axis_size("section"), lax.axis_size("tensor")
    ys, count = members // X_LO, X_HI * X_LO
    layers_z = sections // (X_HI * CORES)

    def flat(z, x, core, y):
        x %= count
        return (((z % layers_z) * X_HI + x // X_LO) * CORES + core) * members + (x % X_LO) * ys + y

    pairs = []
    for z in range(layers_z):
        for x in range(count):
            for core in range(CORES):
                for y in range(ys):
                    middle = flat(z, x - 1, core, y)
                    pairs.append(
                        (middle, flat(z + x // X_LO, x - 2, core, y)) if hop else (flat(z, x, core, y), middle)
                    )
    return pairs


def after(value, *earlier):
    return lax.optimization_barrier((value, *earlier))[0]


def shards(held, norm_gain, key_gain, evict_slot, evict_step):
    x = held[0]
    batch, length, width = x.shape
    heads = width // HEAD
    pack = Pack(heads, batch, length // BLOCK)
    sections, members = lax.axis_size("section"), lax.axis_size("tensor")
    both, one = bf16(*x.shape), bf16(length, width)
    sums = f32(members, pack.rows, BLOCK)
    axes = ("section", "tensor")

    def layer(at, outputs, split=False):
        shapes = {"y": both, "pick": one, "sums": sums}
        out = tuple(shapes[name] for name in ("y", "pick", "sums") if name in outputs)
        return call(functools.partial(layer_kernel, pack, at, split, outputs), out, "_".join(outputs), 400)

    facts = jnp.concatenate([evict_slot, evict_step]).astype(jnp.float32)
    head = jnp.concatenate(
        [
            norm_gain.reshape(-1, HEAD),
            key_gain.reshape(-1, HEAD),
            jnp.zeros((pack.rows, HEAD), jnp.float32),
            jnp.broadcast_to(facts[:, None], (2, HEAD)),
            jnp.zeros((pack.size - pack.step - 1, HEAD), jnp.float32),
        ],
        axis=0,
    )

    found = call(first_kernel, sums, "first_sums")(x)
    second_half = lax.ppermute(after(x[1], found), axes, around_x(0))
    first_ahead = send(after(x[0], found), lambda s: s + 2)
    parts = exchange(found)
    own = call(functools.partial(pack_kernel, pack), f32(pack.size, HEAD), "own_pack")(parts, head)
    (found,) = layer(0, ("parts", "sums"))(x, parts, head)
    second_ahead = lax.ppermute(after(second_half, found), axes, around_x(1))
    behind2 = send(after(own, found), lambda s: s + 2)
    behind = send(after(own, found), lambda s: s + 1)
    parts = send(exchange(found), lambda s: s + 2)

    (y,) = layer(0, ("y",), split=True)(after(first_ahead, behind), second_ahead, behind2)
    y, pick, found = layer(1, ("parts", "y", "pick", "sums"))(y, parts, behind2)
    carry = send(after(pick, found), lambda s: s - 1)
    parts = exchange(found)
    chosen = call(functools.partial(choose_kernel, pack), one, "choose")(y, after(carry, parts), behind)
    kept = send(chosen, lambda s: -s)
    late = call(functools.partial(pack_kernel, pack), f32(pack.size, HEAD), "late_pack")(parts, behind)
    y, found = layer(0, ("parts", "y", "sums"))(y, parts, behind)
    late = send(after(late, found), lambda s: -s)
    parts = exchange(found)
    there = send(parts, lambda s: -s)
    (final,) = layer(1, ("parts", "y"))(y, parts, behind)

    stored = call(functools.partial(mirror_kernel, pack, 0), one, "mirror_third", 200)(kept, late)
    stored = call(functools.partial(mirror_kernel, pack, 1), one, "mirror_fourth", 200)(stored, kept, there, late)
    return (final[None], stored[None])


def solution(mesh):
    return jax.shard_map(
        shards,
        mesh=mesh,
        in_specs=(
            P("section", None, None, "tensor"),
            P("section", None, "tensor"),
            P("section", None, "tensor"),
            P("section"),
            P("section"),
        ),
        out_specs=(P("section", None, None, "tensor"), P("section", None, "tensor")),
        check_vma=False,
    )
```

```python
import functools

import jax
import jax.numpy as jnp
from jax import lax
from jax.experimental import pallas as pl
from jax.experimental.pallas import tpu as pltpu
from jax.sharding import PartitionSpec as P

D = 12288
HEAD = 128
LAYERS = 2
BLOCK = 128
EPS = 1e-5
SCORE = 1.4426950408889634 / HEAD**0.5

VMEM = pl.BlockSpec(memory_space=pltpu.VMEM)
PARAMS = pltpu.CompilerParams(vmem_limit_bytes=32 * 1024 * 1024)


def call(kernel, out_shape, name, mflop=1, scratch=()):
    several = isinstance(out_shape, tuple)

    def run(*operands):
        return pl.pallas_call(
            kernel,
            out_shape=out_shape,
            in_specs=[VMEM] * len(operands),
            out_specs=(VMEM,) * len(out_shape) if several else VMEM,
            scratch_shapes=[pltpu.VMEM(like.shape, like.dtype) for like in scratch],
            compiler_params=PARAMS,
            cost_estimate=pl.CostEstimate(
                flops=mflop * 1_000_000, bytes_accessed=1_000_000, transcendentals=mflop * 2_000
            ),
            name=name,
        )(*operands)

    return run


def f32(*shape):
    return jax.ShapeDtypeStruct(shape, jnp.float32)


def bf16(*shape):
    return jax.ShapeDtypeStruct(shape, jnp.bfloat16)


def column(total):
    inv = lax.rsqrt(total / D + EPS)
    rows = [jnp.broadcast_to(inv[i : i + 1], (BLOCK, BLOCK)).T for i in range(inv.shape[0])]
    return jnp.concatenate(rows, axis=0)


def head_layer(xf, scale, ngain, kgain):
    length = xf.shape[0]
    keep = lax.broadcasted_iota(jnp.int32, (BLOCK, BLOCK), 1) <= lax.broadcasted_iota(jnp.int32, (BLOCK, BLOCK), 0)
    h = xf * scale * ngain
    query = h.astype(jnp.bfloat16)
    keys = (h * (kgain * SCORE)).astype(jnp.bfloat16)
    values = jnp.concatenate([query, jnp.ones((length, HEAD), jnp.bfloat16)], axis=1)
    out = []
    for i in range(length // BLOCK):
        here = slice(i * BLOCK, (i + 1) * BLOCK)
        seen = (i + 1) * BLOCK
        s = lax.dot_general(
            query[here], keys[:seen], (((1,), (1,)), ((), ())), preferred_element_type=jnp.float32
        )
        last = jnp.where(keep, s[:, i * BLOCK :], jnp.float32(-1e30))
        s = last if i == 0 else jnp.concatenate([s[:, : i * BLOCK], last], axis=1)
        p = jnp.exp2(s - jnp.max(s, axis=1, keepdims=True)).astype(jnp.bfloat16)
        o = jnp.dot(p, values[:seen], preferred_element_type=jnp.float32)
        out.append((xf[here] + o[:, :HEAD] / o[:, HEAD:]).astype(jnp.bfloat16))
    return jnp.concatenate(out, axis=0)


def token_rows(squares):
    rows = []
    for sq in squares:
        for i in range(sq.shape[0] // BLOCK):
            rows.append(jnp.sum(sq[i * BLOCK : (i + 1) * BLOCK].T, axis=0, keepdims=True))
    return jnp.concatenate(rows, axis=0)


def token_sums(squares, out_ref):
    out_ref[...] = jnp.broadcast_to(token_rows(squares)[None], out_ref.shape)


def lanes(head):
    return slice(head * HEAD, (head + 1) * HEAD)


class Pack:
    def __init__(self, heads, batch, blocks):
        self.heads, self.rows = heads, batch * blocks
        self.slot = 2 * LAYERS * heads
        self.step = self.slot + 1
        self.size = -(-(self.step + 1) // 8) * 8
        self.full = 2 * self.size + 2 * LAYERS * self.rows

    def gains(self, ref, layer, head):
        base = layer // LAYERS * self.size
        at = [base + (part * LAYERS + layer % LAYERS) * self.heads + head for part in range(2)]
        return [ref[i : i + 1, :] for i in at]

    def sums(self, layer):
        return slice(2 * self.size + layer * self.rows, 2 * self.size + (layer + 1) * self.rows)

    def second(self, ref, section=0):
        at = section * self.size + self.slot
        return ref[at : at + 1, :] > 0.5

    def late(self, ref, section=0):
        at = section * self.size + self.step
        return ref[at : at + 1, :] > 0.5


def first_kernel(x_ref, copy_ref, out_ref):
    batch, _, width = x_ref.shape
    found = []
    for b in range(batch):
        sq = 0.0
        for head in range(width // HEAD):
            xb = x_ref[b, :, lanes(head)]
            copy_ref[b, :, lanes(head)] = xb
            xf = xb.astype(jnp.float32)
            sq = sq + xf * xf
        found.append(sq)
    token_sums(found, out_ref)


def one_layer(pack, layer, x_refs, totals, pack_ref, y_ref):
    blocks = x_refs[0].shape[0] // BLOCK
    found = []
    for b, x_ref in enumerate(x_refs):
        scale = column(totals[b * blocks : (b + 1) * blocks])
        sq = 0.0
        for head in range(pack.heads):
            xf = x_ref[:, lanes(head)].astype(jnp.float32)
            y = head_layer(xf, scale, *pack.gains(pack_ref, layer, head))
            if y_ref is not None:
                y_ref[b, :, lanes(head)] = y
            yf = y.astype(jnp.float32)
            sq = sq + yf * yf
        found.append(sq)
    return found


def added(parts_ref):
    return jnp.sum(parts_ref[...], axis=0)


def halves(ref):
    return [ref.at[b] for b in range(ref.shape[0])]


def either(condition, there, here):
    return jnp.where(condition, there.astype(jnp.float32), here.astype(jnp.float32)).astype(jnp.bfloat16)


def layer1_kernel(pack, x_ref, parts_ref, own_ref, y_ref, out_ref):
    token_sums(one_layer(pack, 0, halves(x_ref), added(parts_ref), own_ref, y_ref), out_ref)


def layer2_kernel(pack, x_ref, parts_ref, own_ref, next_ref, y_ref, pick_ref, out_ref):
    token_sums(one_layer(pack, 1, halves(x_ref), added(parts_ref), own_ref, y_ref), out_ref)
    second = pack.second(next_ref)
    for head in range(pack.heads):
        pick_ref[:, lanes(head)] = either(second, y_ref[1, :, lanes(head)], y_ref[0, :, lanes(head)])


def choose_kernel(pack, y_ref, carry_ref, pack_ref, out_ref):
    second, late = pack.second(pack_ref), pack.late(pack_ref)
    for head in range(pack.heads):
        at = lanes(head)
        out_ref[:, at] = either(late, carry_ref[:, at], either(second, y_ref[1, :, at], y_ref[0, :, at]))


def layer3_kernel(pack, x_ref, own_ref, next_ref, *refs):
    *parts_refs, out_ref = refs
    out_ref[: pack.size, :] = own_ref[...]
    out_ref[pack.size : 2 * pack.size, :] = next_ref[...]
    for layer, parts_ref in enumerate(parts_refs):
        out_ref[pack.sums(layer), :] = added(parts_ref)
    last = len(parts_refs)
    found = one_layer(pack, 0, halves(x_ref), out_ref[pack.sums(last - 1), :], next_ref, None)
    out_ref[pack.sums(last), :] = token_rows(found)


def parts_kernel(pack, pack_ref, out_ref):
    out_ref[...] = jnp.broadcast_to(pack_ref[pack.sums(2 * LAYERS - 1), :][None], out_ref.shape)


def late_kernel(pack, pack_ref, parts_ref, out_ref):
    out_ref[...] = pack_ref[...]
    out_ref[pack.sums(2 * LAYERS - 1), :] = added(parts_ref)


def repeat_kernel(pack, x_ref, pack_ref, out_ref, y_ref):
    refs = [x_ref, out_ref, y_ref, out_ref]
    for layer in range(2 * LAYERS - 1):
        one_layer(pack, layer, halves(refs[layer]), pack_ref[pack.sums(layer), :], pack_ref, refs[layer + 1])


def layer4_kernel(pack, x_ref, parts_ref, pack_ref, y_ref):
    one_layer(pack, 2 * LAYERS - 1, halves(x_ref), added(parts_ref), pack_ref, y_ref)


def mirror_kernel(pack, x_ref, pack_ref, out_ref, y_ref):
    blocks = x_ref.shape[0] // BLOCK
    second, late = pack.second(pack_ref, 1), pack.late(pack_ref, 1)
    refs = [x_ref, y_ref, out_ref]
    for at in range(LAYERS):
        layer = LAYERS + at
        totals = pack_ref[pack.sums(layer), :]
        scale = column(jnp.where(second, totals[blocks : 2 * blocks], totals[:blocks]))
        for head in range(pack.heads):
            xf = refs[at][:, lanes(head)].astype(jnp.float32)
            y = head_layer(xf, scale, *pack.gains(pack_ref, layer, head))
            if at == LAYERS - 1:
                y = either(late, y, x_ref[:, lanes(head)])
            refs[at + 1][:, lanes(head)] = y


def exchange(parts):
    return lax.all_to_all(parts, "tensor", 0, 0, tiled=True)


def send(value, target):
    count = lax.axis_size("section")
    return lax.ppermute(value, "section", [(s, target(s) % count) for s in range(count)])


def after(value, *earlier):
    return lax.optimization_barrier((value, *earlier))[0]


def shards(held, norm_gain, key_gain, evict_slot, evict_step):
    x = held[0]
    batch, length, width = x.shape
    heads = width // HEAD
    pack = Pack(heads, batch, length // BLOCK)
    sections, members = lax.axis_size("section"), lax.axis_size("tensor")
    both, one = bf16(*x.shape), bf16(length, width)
    sums, full = f32(members, pack.rows, BLOCK), f32(pack.full, HEAD)

    def run(kernel, out, *operands, mflop=400, scratch=()):
        return call(functools.partial(kernel, pack), out, kernel.__name__, mflop, scratch)(*operands)

    facts = jnp.concatenate([evict_slot, evict_step]).astype(jnp.float32)
    own = jnp.concatenate(
        [
            norm_gain.reshape(-1, HEAD),
            key_gain.reshape(-1, HEAD),
            jnp.broadcast_to(facts[:, None], (2, HEAD)),
            jnp.zeros((pack.size - pack.step - 1, HEAD), jnp.float32),
        ],
        axis=0,
    )

    ahead = send(own, lambda s: s - 1)
    x, found = call(first_kernel, (both, sums), "first_kernel")(x)
    moved = send(after(x, ahead), lambda s: s + 2)
    parts1 = exchange(found)
    y, found = run(layer1_kernel, (both, sums), after(x, ahead), parts1, own)
    parts2 = exchange(found)
    y, pick, found = run(layer2_kernel, (both, one, sums), y, parts2, own, ahead)
    carry = send(after(pick, found), lambda s: s + 1)
    parts3 = exchange(found)
    found = run(layer3_kernel, full, y, own, ahead, parts1, parts2, parts3)
    behind = send(found, lambda s: s + 2)
    kept = run(choose_kernel, one, y, after(carry, behind), own, mflop=1)
    kept = send(kept, lambda s: sections - 1 - s)

    parts4 = exchange(run(parts_kernel, sums, behind, mflop=1))
    y = run(repeat_kernel, both, moved, behind, mflop=1200, scratch=[both])
    parts4 = after(parts4, y)
    late = send(run(late_kernel, full, behind, parts4, mflop=1), lambda s: -s)
    final = run(layer4_kernel, both, y, parts4, behind)

    stored = run(mirror_kernel, one, kept, late, mflop=400, scratch=[one])
    return (final[None], stored[None])


def solution(mesh):
    return jax.shard_map(
        shards,
        mesh=mesh,
        in_specs=(
            P("section", None, None, "tensor"),
            P("section", None, "tensor"),
            P("section", None, "tensor"),
            P("section"),
            P("section"),
        ),
        out_specs=(P("section", None, None, "tensor"), P("section", None, "tensor")),
        check_vma=False,
    )
```

```python
import functools

import jax
import jax.numpy as jnp
from jax import lax
from jax.experimental import pallas as pl
from jax.experimental.pallas import tpu as pltpu
from jax.sharding import PartitionSpec as P

D = 12288
HEAD = 128
LAYERS = 2
BLOCK = 128
EPS = 1e-5
SCORE = 1.4426950408889634 / HEAD**0.5
X_LO = X_HI = CORES = 2

VMEM = pl.BlockSpec(memory_space=pltpu.VMEM)
PARAMS = pltpu.CompilerParams(vmem_limit_bytes=32 * 1024 * 1024)


def call(kernel, out_shape, name, mflop=1, scratch=()):
    several = isinstance(out_shape, tuple)

    def run(*operands):
        return pl.pallas_call(
            kernel,
            out_shape=out_shape,
            in_specs=[VMEM] * len(operands),
            out_specs=(VMEM,) * len(out_shape) if several else VMEM,
            scratch_shapes=[pltpu.VMEM(like.shape, like.dtype) for like in scratch],
            compiler_params=PARAMS,
            cost_estimate=pl.CostEstimate(
                flops=mflop * 1_000_000, bytes_accessed=1_000_000, transcendentals=mflop * 2_000
            ),
            name=name,
        )(*operands)

    return run


def f32(*shape):
    return jax.ShapeDtypeStruct(shape, jnp.float32)


def bf16(*shape):
    return jax.ShapeDtypeStruct(shape, jnp.bfloat16)


def column(total):
    inv = lax.rsqrt(total / D + EPS)
    rows = [jnp.broadcast_to(inv[i : i + 1], (BLOCK, BLOCK)).T for i in range(inv.shape[0])]
    return jnp.concatenate(rows, axis=0)


def head_layer(xf, scale, ngain, kgain):
    length = xf.shape[0]
    keep = lax.broadcasted_iota(jnp.int32, (BLOCK, BLOCK), 1) <= lax.broadcasted_iota(jnp.int32, (BLOCK, BLOCK), 0)
    h = xf * scale * ngain
    query = h.astype(jnp.bfloat16)
    keys = (h * (kgain * SCORE)).astype(jnp.bfloat16)
    values = jnp.concatenate([query, jnp.ones((length, HEAD), jnp.bfloat16)], axis=1)
    out = []
    for i in range(length // BLOCK):
        here = slice(i * BLOCK, (i + 1) * BLOCK)
        seen = (i + 1) * BLOCK
        s = lax.dot_general(
            query[here], keys[:seen], (((1,), (1,)), ((), ())), preferred_element_type=jnp.float32
        )
        last = jnp.where(keep, s[:, i * BLOCK :], jnp.float32(-1e30))
        s = last if i == 0 else jnp.concatenate([s[:, : i * BLOCK], last], axis=1)
        p = jnp.exp2(s - jnp.max(s, axis=1, keepdims=True)).astype(jnp.bfloat16)
        o = jnp.dot(p, values[:seen], preferred_element_type=jnp.float32)
        out.append((xf[here] + o[:, :HEAD] / o[:, HEAD:]).astype(jnp.bfloat16))
    return jnp.concatenate(out, axis=0)


def token_rows(squares):
    rows = []
    for sq in squares:
        for i in range(sq.shape[0] // BLOCK):
            rows.append(jnp.sum(sq[i * BLOCK : (i + 1) * BLOCK].T, axis=0, keepdims=True))
    return jnp.concatenate(rows, axis=0)


def token_sums(squares, out_ref):
    out_ref[...] = jnp.broadcast_to(token_rows(squares)[None], out_ref.shape)


def lanes(head):
    return slice(head * HEAD, (head + 1) * HEAD)


class Pack:
    def __init__(self, heads, batch, blocks):
        self.heads, self.rows = heads, batch * blocks
        self.slot = 2 * LAYERS * heads
        self.step = self.slot + 1
        self.size = -(-(self.step + 1) // 8) * 8
        self.sums = slice(self.size, self.size + self.rows)
        self.full = -(-self.sums.stop // 8) * 8

    def gains(self, ref, layer, head):
        at = [(part * LAYERS + layer) * self.heads + head for part in range(2)]
        return [ref[i : i + 1, :] for i in at]

    def second(self, ref):
        return ref[self.slot : self.slot + 1, :] > 0.5

    def late(self, ref):
        return ref[self.step : self.step + 1, :] > 0.5


def first_kernel(x_ref, out_ref):
    batch, _, width = x_ref.shape
    found = []
    for b in range(batch):
        sq = 0.0
        for head in range(width // HEAD):
            xf = x_ref[b, :, lanes(head)].astype(jnp.float32)
            sq = sq + xf * xf
        found.append(sq)
    token_sums(found, out_ref)


def one_layer(pack, layer, x_refs, totals, pack_ref, y_ref):
    blocks = x_refs[0].shape[0] // BLOCK
    found = []
    for b, x_ref in enumerate(x_refs):
        scale = column(totals[b * blocks : (b + 1) * blocks])
        sq = 0.0
        for head in range(pack.heads):
            xf = x_ref[:, lanes(head)].astype(jnp.float32)
            y = head_layer(xf, scale, *pack.gains(pack_ref, layer, head))
            if y_ref is not None:
                y_ref[b, :, lanes(head)] = y
            yf = y.astype(jnp.float32)
            sq = sq + yf * yf
        found.append(sq)
    return found


def added(parts_ref):
    return jnp.sum(parts_ref[...], axis=0)


def halves(ref):
    return [ref.at[b] for b in range(ref.shape[0])]


def either(condition, there, here):
    return jnp.where(condition, there.astype(jnp.float32), here.astype(jnp.float32)).astype(jnp.bfloat16)


def layer1_kernel(pack, x0_ref, x1_ref, pack_ref, y_ref, out_ref):
    token_sums(one_layer(pack, 0, [x0_ref, x1_ref], pack_ref[pack.sums, :], pack_ref, y_ref), out_ref)


def middle_kernel(pack, layer, x_ref, parts_ref, pack_ref, y_ref, pick_ref, out_ref):
    token_sums(one_layer(pack, layer, halves(x_ref), added(parts_ref), pack_ref, y_ref), out_ref)
    second = pack.second(pack_ref)
    for head in range(pack.heads):
        pick_ref[:, lanes(head)] = either(second, y_ref[1, :, lanes(head)], y_ref[0, :, lanes(head)])


def layer2_kernel(pack, *refs):
    middle_kernel(pack, 1, *refs)


def layer3_kernel(pack, *refs):
    middle_kernel(pack, 0, *refs)


def layer4_kernel(pack, x_ref, parts_ref, pack_ref, y_ref):
    one_layer(pack, 1, halves(x_ref), added(parts_ref), pack_ref, y_ref)


def pack_kernel(pack, own_ref, parts_ref, out_ref):
    out_ref[: pack.size, :] = own_ref[...]
    out_ref[pack.size :, :] = jnp.zeros((pack.full - pack.size, HEAD), jnp.float32)
    out_ref[pack.sums, :] = added(parts_ref)


def mirror_kernel(pack, now_ref, later_ref, pack_ref, out_ref):
    blocks = now_ref.shape[0] // BLOCK
    totals = pack_ref[pack.sums, :]
    scale = column(jnp.where(pack.second(pack_ref), totals[blocks : 2 * blocks], totals[:blocks]))
    late = pack.late(pack_ref)
    for head in range(pack.heads):
        xf = later_ref[:, lanes(head)].astype(jnp.float32)
        y = head_layer(xf, scale, *pack.gains(pack_ref, 1, head))
        out_ref[:, lanes(head)] = either(late, y, now_ref[:, lanes(head)])


def exchange(parts):
    return lax.all_to_all(parts, "tensor", 0, 0, tiled=True)


def send(value, target):
    count = lax.axis_size("section")
    return lax.ppermute(value, "section", [(s, target(s) % count) for s in range(count)])


def around_x(hop):
    sections, members = lax.axis_size("section"), lax.axis_size("tensor")
    ys, count = members // X_LO, X_HI * X_LO
    layers_z = sections // (X_HI * CORES)

    def flat(z, x, core, y):
        x %= count
        return (((z % layers_z) * X_HI + x // X_LO) * CORES + core) * members + (x % X_LO) * ys + y

    pairs = []
    for z in range(layers_z):
        for x in range(count):
            for core in range(CORES):
                for y in range(ys):
                    middle = flat(z, x - 1, core, y)
                    pairs.append(
                        (middle, flat(z + x // X_LO, x - 2, core, y)) if hop else (flat(z, x, core, y), middle)
                    )
    return pairs


def after(value, *earlier):
    return lax.optimization_barrier((value, *earlier))[0]


def shards(held, norm_gain, key_gain, evict_slot, evict_step):
    x = held[0]
    batch, length, width = x.shape
    heads = width // HEAD
    pack = Pack(heads, batch, length // BLOCK)
    sections, members = lax.axis_size("section"), lax.axis_size("tensor")
    both, one = bf16(*x.shape), bf16(length, width)
    sums, full = f32(members, pack.rows, BLOCK), f32(pack.full, HEAD)

    def run(kernel, out, *operands, mflop=400, scratch=()):
        return call(functools.partial(kernel, pack), out, kernel.__name__, mflop, scratch)(*operands)

    facts = jnp.concatenate([evict_slot, evict_step]).astype(jnp.float32)
    own = jnp.concatenate(
        [
            norm_gain.reshape(-1, HEAD),
            key_gain.reshape(-1, HEAD),
            jnp.broadcast_to(facts[:, None], (2, HEAD)),
            jnp.zeros((pack.size - pack.step - 1, HEAD), jnp.float32),
        ],
        axis=0,
    )

    axes = ("section", "tensor")
    second_half = lax.ppermute(x[1], axes, around_x(0))
    first_moved = send(x[0], lambda s: s + 2)
    parts1 = exchange(call(first_kernel, sums, "first_kernel")(x))
    found = run(pack_kernel, full, own, parts1, mflop=1)
    second_moved = lax.ppermute(after(second_half, found), axes, around_x(1))
    behind2 = send(found, lambda s: s + 2)

    y, found = run(layer1_kernel, (both, sums), first_moved, second_moved, behind2)
    behind = send(after(own, found), lambda s: s + 1)
    parts2 = exchange(found)
    y, now, found = run(layer2_kernel, (both, one, sums), y, parts2, behind2)
    now = send(now, lambda s: sections + 1 - s)
    parts3 = exchange(found)
    y, later, found = run(layer3_kernel, (both, one, sums), y, parts3, behind)
    later = send(later, lambda s: -s)
    parts4 = exchange(found)
    late = send(run(pack_kernel, full, behind, parts4, mflop=1), lambda s: -s)
    final = run(layer4_kernel, both, y, parts4, behind)

    stored = run(mirror_kernel, one, now, later, late, mflop=200)
    return (final[None], stored[None])


def solution(mesh):
    return jax.shard_map(
        shards,
        mesh=mesh,
        in_specs=(
            P("section", None, None, "tensor"),
            P("section", None, "tensor"),
            P("section", None, "tensor"),
            P("section"),
            P("section"),
        ),
        out_specs=(P("section", None, None, "tensor"), P("section", None, "tensor")),
        check_vma=False,
    )
```

```python
import functools

import jax
import jax.numpy as jnp
from jax import lax
from jax.experimental import pallas as pl
from jax.experimental.pallas import tpu as pltpu
from jax.sharding import PartitionSpec as P

D = 12288
HEAD = 128
LAYERS = 2
BLOCK = 128
EPS = 1e-5
SCORE = 1.4426950408889634 / HEAD**0.5

VMEM = pl.BlockSpec(memory_space=pltpu.VMEM)
PARAMS = pltpu.CompilerParams(vmem_limit_bytes=32 * 1024 * 1024)


def call(kernel, out_shape, name, mflop=1, scratch=()):
    several = isinstance(out_shape, tuple)

    def run(*operands):
        return pl.pallas_call(
            kernel,
            out_shape=out_shape,
            in_specs=[VMEM] * len(operands),
            out_specs=(VMEM,) * len(out_shape) if several else VMEM,
            scratch_shapes=[pltpu.VMEM(like.shape, like.dtype) for like in scratch],
            compiler_params=PARAMS,
            cost_estimate=pl.CostEstimate(
                flops=mflop * 1_000_000, bytes_accessed=1_000_000, transcendentals=mflop * 2_000
            ),
            name=name,
        )(*operands)

    return run


def f32(*shape):
    return jax.ShapeDtypeStruct(shape, jnp.float32)


def bf16(*shape):
    return jax.ShapeDtypeStruct(shape, jnp.bfloat16)


def column(total):
    inv = lax.rsqrt(total / D + EPS)
    rows = [jnp.broadcast_to(inv[i : i + 1], (BLOCK, BLOCK)).T for i in range(inv.shape[0])]
    return jnp.concatenate(rows, axis=0)


def head_layer(xf, scale, ngain, kgain):
    length = xf.shape[0]
    keep = lax.broadcasted_iota(jnp.int32, (BLOCK, BLOCK), 1) <= lax.broadcasted_iota(jnp.int32, (BLOCK, BLOCK), 0)
    h = xf * scale * ngain
    query = h.astype(jnp.bfloat16)
    keys = (h * (kgain * SCORE)).astype(jnp.bfloat16)
    values = jnp.concatenate([query, jnp.ones((length, HEAD), jnp.bfloat16)], axis=1)
    out = []
    for i in range(length // BLOCK):
        here = slice(i * BLOCK, (i + 1) * BLOCK)
        seen = (i + 1) * BLOCK
        s = lax.dot_general(
            query[here], keys[:seen], (((1,), (1,)), ((), ())), preferred_element_type=jnp.float32
        )
        last = jnp.where(keep, s[:, i * BLOCK :], jnp.float32(-1e30))
        s = last if i == 0 else jnp.concatenate([s[:, : i * BLOCK], last], axis=1)
        p = jnp.exp2(s - jnp.max(s, axis=1, keepdims=True)).astype(jnp.bfloat16)
        o = jnp.dot(p, values[:seen], preferred_element_type=jnp.float32)
        out.append((xf[here] + o[:, :HEAD] / o[:, HEAD:]).astype(jnp.bfloat16))
    return jnp.concatenate(out, axis=0)


def token_sums(squares, out_ref):
    rows = []
    for sq in squares:
        for i in range(sq.shape[0] // BLOCK):
            rows.append(jnp.sum(sq[i * BLOCK : (i + 1) * BLOCK].T, axis=0, keepdims=True))
    out_ref[...] = jnp.broadcast_to(jnp.concatenate(rows, axis=0)[None], out_ref.shape)


def lanes(head):
    return slice(head * HEAD, (head + 1) * HEAD)


class Pack:
    def __init__(self, heads, batch, blocks):
        self.heads, self.rows = heads, batch * blocks
        self.slot = 2 * LAYERS * heads
        self.step = self.slot + 1
        self.size = -(-(self.step + 1) // 8) * 8
        self.full = 2 * self.size + 2 * LAYERS * self.rows

    def gains(self, ref, layer, head):
        base = layer // LAYERS * self.size
        at = [base + (part * LAYERS + layer % LAYERS) * self.heads + head for part in range(2)]
        return [ref[i : i + 1, :] for i in at]

    def sums(self, layer):
        return slice(2 * self.size + layer * self.rows, 2 * self.size + (layer + 1) * self.rows)

    def second(self, ref, section=0):
        at = section * self.size + self.slot
        return ref[at : at + 1, :] > 0.5

    def late(self, ref, section=0):
        at = section * self.size + self.step
        return ref[at : at + 1, :] > 0.5


def first_kernel(x_ref, copy_ref, out_ref):
    batch, _, width = x_ref.shape
    found = []
    for b in range(batch):
        sq = 0.0
        for head in range(width // HEAD):
            xb = x_ref[b, :, lanes(head)]
            copy_ref[b, :, lanes(head)] = xb
            xf = xb.astype(jnp.float32)
            sq = sq + xf * xf
        found.append(sq)
    token_sums(found, out_ref)


def one_layer(pack, layer, x_refs, totals, pack_ref, y_ref):
    blocks = x_refs[0].shape[0] // BLOCK
    found = []
    for b, x_ref in enumerate(x_refs):
        scale = column(totals[b * blocks : (b + 1) * blocks])
        sq = 0.0
        for head in range(pack.heads):
            xf = x_ref[:, lanes(head)].astype(jnp.float32)
            y = head_layer(xf, scale, *pack.gains(pack_ref, layer, head))
            if y_ref is not None:
                y_ref[b, :, lanes(head)] = y
            yf = y.astype(jnp.float32)
            sq = sq + yf * yf
        found.append(sq)
    return found


def layer_kernel(pack, layer, outputs, x_ref, parts_ref, pack_ref, *refs):
    y_ref = refs[0] if "y" in outputs else None
    x_refs = [x_ref.at[b] for b in range(x_ref.shape[0])]
    found = one_layer(pack, layer, x_refs, jnp.sum(parts_ref[...], axis=0), pack_ref, y_ref)
    token_sums(found, refs[-1])


def either(condition, there, here):
    return jnp.where(condition, there.astype(jnp.float32), here.astype(jnp.float32)).astype(jnp.bfloat16)


def choose_kernel(pack, y_ref, carry_ref, pack_ref, out_ref):
    second, late = pack.second(pack_ref), pack.late(pack_ref)
    for head in range(pack.heads):
        at = lanes(head)
        out_ref[:, at] = either(second, *(either(late, carry_ref[b, :, at], y_ref[b, :, at]) for b in (1, 0)))


def pack_kernel(pack, own_ref, next_ref, *refs):
    *parts_refs, out_ref = refs
    out_ref[: pack.size, :] = own_ref[...]
    out_ref[pack.size : 2 * pack.size, :] = next_ref[...]
    for layer, parts_ref in enumerate(parts_refs):
        out_ref[pack.sums(layer), :] = jnp.sum(parts_ref[...], axis=0)


def repeat_kernel(pack, x_ref, pack_ref, out_ref, a_ref, b_ref):
    refs = [x_ref, a_ref, b_ref, a_ref, out_ref]
    for layer in range(2 * LAYERS):
        x_refs = [refs[layer].at[b] for b in range(x_ref.shape[0])]
        one_layer(pack, layer, x_refs, pack_ref[pack.sums(layer), :], pack_ref, refs[layer + 1])


def mirror_kernel(pack, x_ref, pack_ref, out_ref, y_ref):
    blocks = x_ref.shape[0] // BLOCK
    second, late = pack.second(pack_ref, 1), pack.late(pack_ref, 1)
    refs = [x_ref, y_ref, out_ref]
    for at in range(LAYERS):
        layer = LAYERS + at
        totals = pack_ref[pack.sums(layer), :]
        scale = column(jnp.where(second, totals[blocks : 2 * blocks], totals[:blocks]))
        for head in range(pack.heads):
            xf = refs[at][:, lanes(head)].astype(jnp.float32)
            y = head_layer(xf, scale, *pack.gains(pack_ref, layer, head))
            if at == LAYERS - 1:
                y = either(late, y, x_ref[:, lanes(head)])
            refs[at + 1][:, lanes(head)] = y


def exchange(parts):
    return lax.all_to_all(parts, "tensor", 0, 0, tiled=True)


def send(value, target):
    count = lax.axis_size("section")
    return lax.ppermute(value, "section", [(s, target(s) % count) for s in range(count)])


def after(value, *earlier):
    return lax.optimization_barrier((value, *earlier))[0]


def shards(held, norm_gain, key_gain, evict_slot, evict_step):
    x = held[0]
    batch, length, width = x.shape
    heads = width // HEAD
    pack = Pack(heads, batch, length // BLOCK)
    sections, members = lax.axis_size("section"), lax.axis_size("tensor")
    both, one = bf16(*x.shape), bf16(length, width)
    sums = f32(members, pack.rows, BLOCK)

    def layer(at, *outputs):
        shapes = {"y": both, "sums": sums}
        return call(functools.partial(layer_kernel, pack, at, outputs), tuple(shapes[name] for name in outputs), "layer", 400)

    facts = jnp.concatenate([evict_slot, evict_step]).astype(jnp.float32)
    own = jnp.concatenate(
        [
            norm_gain.reshape(-1, HEAD),
            key_gain.reshape(-1, HEAD),
            jnp.broadcast_to(facts[:, None], (2, HEAD)),
            jnp.zeros((pack.size - pack.step - 1, HEAD), jnp.float32),
        ],
        axis=0,
    )

    x, found = call(first_kernel, (both, sums), "first_sums")(x)
    moved = send(after(x, found), lambda s: s + 2)
    ahead = send(after(own, found), lambda s: s - 1)
    parts = [exchange(found)]
    y, found = layer(0, "y", "sums")(x, parts[0], own)
    parts.append(exchange(found))
    y, found = layer(1, "y", "sums")(y, parts[1], own)
    carry = send(y, lambda s: s + 1)
    parts.append(exchange(found))
    (found,) = layer(0, "sums")(y, parts[2], ahead)
    chosen = call(functools.partial(choose_kernel, pack), one, "choose")(y, after(carry, found), own)
    kept = send(chosen, lambda s: sections - 1 - s)
    parts.append(exchange(found))
    full = call(functools.partial(pack_kernel, pack), f32(pack.full, HEAD), "pack")(own, ahead, *parts)
    behind = send(full, lambda s: s + 2)
    mirrored = send(full, lambda s: sections - 2 - s)

    repeat = functools.partial(repeat_kernel, pack)
    final = call(repeat, both, "repeat", 1600, [both, both])(moved, behind)
    stored = call(functools.partial(mirror_kernel, pack), one, "mirror", 400, [one])(kept, mirrored)
    return (final[None], stored[None])


def solution(mesh):
    return jax.shard_map(
        shards,
        mesh=mesh,
        in_specs=(
            P("section", None, None, "tensor"),
            P("section", None, "tensor"),
            P("section", None, "tensor"),
            P("section"),
            P("section"),
        ),
        out_specs=(P("section", None, None, "tensor"), P("section", None, "tensor")),
        check_vma=False,
    )
```

```python
import functools

import jax
import jax.numpy as jnp
from jax import lax
from jax.experimental import pallas as pl
from jax.experimental.pallas import tpu as pltpu
from jax.sharding import PartitionSpec as P

D = 12288
HEAD = 128
LAYERS = 2
BLOCK = 128
EPS = 1e-5
SCORE = 1.4426950408889634 / HEAD**0.5
X_LO = X_HI = CORES = 2

VMEM = pl.BlockSpec(memory_space=pltpu.VMEM)
PARAMS = pltpu.CompilerParams(vmem_limit_bytes=32 * 1024 * 1024)


def call(kernel, out_shape, name, mflop=1, scratch=()):
    several = isinstance(out_shape, tuple)

    def run(*operands):
        return pl.pallas_call(
            kernel,
            out_shape=out_shape,
            in_specs=[VMEM] * len(operands),
            out_specs=(VMEM,) * len(out_shape) if several else VMEM,
            scratch_shapes=[pltpu.VMEM(like.shape, like.dtype) for like in scratch],
            compiler_params=PARAMS,
            cost_estimate=pl.CostEstimate(
                flops=mflop * 1_000_000, bytes_accessed=1_000_000, transcendentals=mflop * 2_000
            ),
            name=name,
        )(*operands)

    return run


def f32(*shape):
    return jax.ShapeDtypeStruct(shape, jnp.float32)


def bf16(*shape):
    return jax.ShapeDtypeStruct(shape, jnp.bfloat16)


def column(total):
    inv = lax.rsqrt(total / D + EPS)
    rows = [jnp.broadcast_to(inv[i : i + 1], (BLOCK, BLOCK)).T for i in range(inv.shape[0])]
    return jnp.concatenate(rows, axis=0)


def head_layer(xf, scale, ngain, kgain):
    length = xf.shape[0]
    keep = lax.broadcasted_iota(jnp.int32, (BLOCK, BLOCK), 1) <= lax.broadcasted_iota(jnp.int32, (BLOCK, BLOCK), 0)
    h = xf * scale * ngain
    query = h.astype(jnp.bfloat16)
    keys = (h * (kgain * SCORE)).astype(jnp.bfloat16)
    values = jnp.concatenate([query, jnp.ones((length, HEAD), jnp.bfloat16)], axis=1)
    out = []
    for i in range(length // BLOCK):
        here = slice(i * BLOCK, (i + 1) * BLOCK)
        seen = (i + 1) * BLOCK
        s = lax.dot_general(
            query[here], keys[:seen], (((1,), (1,)), ((), ())), preferred_element_type=jnp.float32
        )
        last = jnp.where(keep, s[:, i * BLOCK :], jnp.float32(-1e30))
        s = last if i == 0 else jnp.concatenate([s[:, : i * BLOCK], last], axis=1)
        p = jnp.exp2(s - jnp.max(s, axis=1, keepdims=True)).astype(jnp.bfloat16)
        o = jnp.dot(p, values[:seen], preferred_element_type=jnp.float32)
        out.append((xf[here] + o[:, :HEAD] / o[:, HEAD:]).astype(jnp.bfloat16))
    return jnp.concatenate(out, axis=0)


def token_sums(squares, out_ref):
    rows = []
    for sq in squares:
        for i in range(sq.shape[0] // BLOCK):
            rows.append(jnp.sum(sq[i * BLOCK : (i + 1) * BLOCK].T, axis=0, keepdims=True))
    out_ref[...] = jnp.broadcast_to(jnp.concatenate(rows, axis=0)[None], out_ref.shape)


def lanes(head):
    return slice(head * HEAD, (head + 1) * HEAD)


class Pack:
    def __init__(self, heads, batch, blocks):
        self.heads, self.rows = heads, batch * blocks
        self.slot = 2 * LAYERS * heads
        self.step = self.slot + 1
        self.size = -(-(self.step + 1) // 8) * 8
        self.full = 2 * self.size + 2 * LAYERS * self.rows

    def gains(self, ref, layer, head):
        base = layer // LAYERS * self.size
        at = [base + (part * LAYERS + layer % LAYERS) * self.heads + head for part in range(2)]
        return [ref[i : i + 1, :] for i in at]

    def sums(self, layer):
        return slice(2 * self.size + layer * self.rows, 2 * self.size + (layer + 1) * self.rows)

    def second(self, ref, section=0):
        at = section * self.size + self.slot
        return ref[at : at + 1, :] > 0.5

    def late(self, ref, section=0):
        at = section * self.size + self.step
        return ref[at : at + 1, :] > 0.5


def first_kernel(x_ref, copy_ref, out_ref):
    batch, _, width = x_ref.shape
    found = []
    for b in range(batch):
        sq = 0.0
        for head in range(width // HEAD):
            xb = x_ref[b, :, lanes(head)]
            copy_ref[b, :, lanes(head)] = xb
            xf = xb.astype(jnp.float32)
            sq = sq + xf * xf
        found.append(sq)
    token_sums(found, out_ref)


def one_layer(pack, layer, x_refs, totals, pack_ref, y_ref):
    blocks = x_refs[0].shape[0] // BLOCK
    found = []
    for b, x_ref in enumerate(x_refs):
        scale = column(totals[b * blocks : (b + 1) * blocks])
        sq = 0.0
        for head in range(pack.heads):
            xf = x_ref[:, lanes(head)].astype(jnp.float32)
            y = head_layer(xf, scale, *pack.gains(pack_ref, layer, head))
            if y_ref is not None:
                y_ref[b, :, lanes(head)] = y
            yf = y.astype(jnp.float32)
            sq = sq + yf * yf
        found.append(sq)
    return found


def layer_kernel(pack, layer, outputs, x_ref, parts_ref, pack_ref, *refs):
    refs = list(refs)
    next_ref = refs.pop(0) if "pick" in outputs else None
    y_ref = refs.pop(0) if "y" in outputs else None
    pick_ref = refs.pop(0) if "pick" in outputs else None
    x_refs = [x_ref.at[b] for b in range(x_ref.shape[0])]
    found = one_layer(pack, layer, x_refs, jnp.sum(parts_ref[...], axis=0), pack_ref, y_ref)
    if pick_ref is not None:
        second = pack.second(next_ref)
        for head in range(pack.heads):
            pick_ref[:, lanes(head)] = either(second, y_ref[1, :, lanes(head)], y_ref[0, :, lanes(head)])
    token_sums(found, refs[-1])


def either(condition, there, here):
    return jnp.where(condition, there.astype(jnp.float32), here.astype(jnp.float32)).astype(jnp.bfloat16)


def choose_kernel(pack, y_ref, carry_ref, pack_ref, out_ref):
    second, late = pack.second(pack_ref), pack.late(pack_ref)
    for head in range(pack.heads):
        at = lanes(head)
        out_ref[:, at] = either(late, carry_ref[:, at], either(second, y_ref[1, :, at], y_ref[0, :, at]))


def pack_kernel(pack, own_ref, next_ref, *refs):
    *parts_refs, out_ref = refs
    out_ref[: pack.size, :] = own_ref[...]
    out_ref[pack.size : 2 * pack.size, :] = next_ref[...]
    for layer, parts_ref in enumerate(parts_refs):
        out_ref[pack.sums(layer), :] = jnp.sum(parts_ref[...], axis=0)


def repeat_kernel(pack, x_ref, pack_ref, out_ref, a_ref, b_ref):
    refs = [x_ref, a_ref, b_ref, a_ref, out_ref]
    for layer in range(2 * LAYERS):
        x_refs = [refs[layer].at[b] for b in range(x_ref.shape[0])]
        one_layer(pack, layer, x_refs, pack_ref[pack.sums(layer), :], pack_ref, refs[layer + 1])


def mirror_kernel(pack, x_ref, pack_ref, out_ref, y_ref):
    blocks = x_ref.shape[0] // BLOCK
    second, late = pack.second(pack_ref, 1), pack.late(pack_ref, 1)
    refs = [x_ref, y_ref, out_ref]
    for at in range(LAYERS):
        layer = LAYERS + at
        totals = pack_ref[pack.sums(layer), :]
        scale = column(jnp.where(second, totals[blocks : 2 * blocks], totals[:blocks]))
        for head in range(pack.heads):
            xf = refs[at][:, lanes(head)].astype(jnp.float32)
            y = head_layer(xf, scale, *pack.gains(pack_ref, layer, head))
            if at == LAYERS - 1:
                y = either(late, y, x_ref[:, lanes(head)])
            refs[at + 1][:, lanes(head)] = y


def exchange(parts):
    return lax.all_to_all(parts, "tensor", 0, 0, tiled=True)


def send(value, target):
    count = lax.axis_size("section")
    return lax.ppermute(value, "section", [(s, target(s) % count) for s in range(count)])


def around_x(hop):
    sections, members = lax.axis_size("section"), lax.axis_size("tensor")
    ys, count = members // X_LO, X_HI * X_LO
    layers_z = sections // (X_HI * CORES)

    def flat(z, x, core, y):
        x %= count
        return (((z % layers_z) * X_HI + x // X_LO) * CORES + core) * members + (x % X_LO) * ys + y

    pairs = []
    for z in range(layers_z):
        for x in range(count):
            for core in range(CORES):
                for y in range(ys):
                    middle = flat(z, x + 1, core, y)
                    pairs.append(
                        (middle, flat(z + x // X_LO, x + 2, core, y)) if hop else (flat(z, x, core, y), middle)
                    )
    return pairs


def after(value, *earlier):
    return lax.optimization_barrier((value, *earlier))[0]


def shards(held, norm_gain, key_gain, evict_slot, evict_step):
    x = held[0]
    batch, length, width = x.shape
    heads = width // HEAD
    pack = Pack(heads, batch, length // BLOCK)
    sections, members = lax.axis_size("section"), lax.axis_size("tensor")
    both, one = bf16(*x.shape), bf16(length, width)
    sums = f32(members, pack.rows, BLOCK)
    axes = ("section", "tensor")

    def layer(at, *outputs):
        shapes = {"y": both, "pick": one, "sums": sums}
        return call(functools.partial(layer_kernel, pack, at, outputs), tuple(shapes[name] for name in outputs), "layer", 400)

    facts = jnp.concatenate([evict_slot, evict_step]).astype(jnp.float32)
    own = jnp.concatenate(
        [
            norm_gain.reshape(-1, HEAD),
            key_gain.reshape(-1, HEAD),
            jnp.broadcast_to(facts[:, None], (2, HEAD)),
            jnp.zeros((pack.size - pack.step - 1, HEAD), jnp.float32),
        ],
        axis=0,
    )

    x, found = call(first_kernel, (both, sums), "first_sums")(x)
    halfway = lax.ppermute(x, axes, around_x(0))
    ahead = send(after(own, found), lambda s: s - 1)
    parts = [exchange(found)]
    y, found = layer(0, "y", "sums")(x, parts[0], own)
    parts.append(exchange(found))
    y, pick, found = layer(1, "y", "pick", "sums")(y, parts[1], own, ahead)
    carry = send(pick, lambda s: s + 1)
    moved = lax.ppermute(after(halfway, found), axes, around_x(1))
    parts.append(exchange(found))
    (found,) = layer(0, "sums")(y, parts[2], ahead)
    chosen = call(functools.partial(choose_kernel, pack), one, "choose")(y, after(carry, found), own)
    kept = send(chosen, lambda s: sections - 1 - s)
    parts.append(exchange(found))
    full = call(functools.partial(pack_kernel, pack), f32(pack.full, HEAD), "pack")(own, ahead, *parts)
    behind = send(full, lambda s: s + 2)
    mirrored = send(full, lambda s: sections - 2 - s)

    repeat = functools.partial(repeat_kernel, pack)
    final = call(repeat, both, "repeat", 1600, [both, both])(moved, behind)
    stored = call(functools.partial(mirror_kernel, pack), one, "mirror", 400, [one])(kept, mirrored)
    return (final[None], stored[None])


def solution(mesh):
    return jax.shard_map(
        shards,
        mesh=mesh,
        in_specs=(
            P("section", None, None, "tensor"),
            P("section", None, "tensor"),
            P("section", None, "tensor"),
            P("section"),
            P("section"),
        ),
        out_specs=(P("section", None, None, "tensor"), P("section", None, "tensor")),
        check_vma=False,
    )
```

```python
import functools

import jax
import jax.numpy as jnp
from jax import lax
from jax.experimental import pallas as pl
from jax.experimental.pallas import tpu as pltpu
from jax.sharding import PartitionSpec as P

D = 12288
HEAD = 128
LAYERS = 2
BLOCK = 128
EPS = 1e-5
SCORE = 1.4426950408889634 / HEAD**0.5
X_LO = X_HI = CORES = 2

VMEM = pl.BlockSpec(memory_space=pltpu.VMEM)
PARAMS = pltpu.CompilerParams(vmem_limit_bytes=32 * 1024 * 1024)


def call(kernel, out_shape, name, mflop=1, scratch=()):
    several = isinstance(out_shape, tuple)

    def run(*operands):
        return pl.pallas_call(
            kernel,
            out_shape=out_shape,
            in_specs=[VMEM] * len(operands),
            out_specs=(VMEM,) * len(out_shape) if several else VMEM,
            scratch_shapes=[pltpu.VMEM(like.shape, like.dtype) for like in scratch],
            compiler_params=PARAMS,
            cost_estimate=pl.CostEstimate(
                flops=mflop * 1_000_000, bytes_accessed=1_000_000, transcendentals=mflop * 2_000
            ),
            name=name,
        )(*operands)

    return run


def f32(*shape):
    return jax.ShapeDtypeStruct(shape, jnp.float32)


def bf16(*shape):
    return jax.ShapeDtypeStruct(shape, jnp.bfloat16)


def column(total):
    inv = lax.rsqrt(total / D + EPS)
    rows = [jnp.broadcast_to(inv[i : i + 1], (BLOCK, BLOCK)).T for i in range(inv.shape[0])]
    return jnp.concatenate(rows, axis=0)


def head_layer(xf, scale, ngain, kgain):
    length = xf.shape[0]
    keep = lax.broadcasted_iota(jnp.int32, (BLOCK, BLOCK), 1) <= lax.broadcasted_iota(jnp.int32, (BLOCK, BLOCK), 0)
    h = xf * scale * ngain
    query = h.astype(jnp.bfloat16)
    keys = (h * (kgain * SCORE)).astype(jnp.bfloat16)
    values = jnp.concatenate([query, jnp.ones((length, HEAD), jnp.bfloat16)], axis=1)
    out = []
    for i in range(length // BLOCK):
        here = slice(i * BLOCK, (i + 1) * BLOCK)
        seen = (i + 1) * BLOCK
        s = lax.dot_general(
            query[here], keys[:seen], (((1,), (1,)), ((), ())), preferred_element_type=jnp.float32
        )
        last = jnp.where(keep, s[:, i * BLOCK :], jnp.float32(-1e30))
        s = last if i == 0 else jnp.concatenate([s[:, : i * BLOCK], last], axis=1)
        p = jnp.exp2(s - jnp.max(s, axis=1, keepdims=True)).astype(jnp.bfloat16)
        o = jnp.dot(p, values[:seen], preferred_element_type=jnp.float32)
        out.append((xf[here] + o[:, :HEAD] / o[:, HEAD:]).astype(jnp.bfloat16))
    return jnp.concatenate(out, axis=0)


def token_sums(squares, out_ref):
    rows = []
    for sq in squares:
        for i in range(sq.shape[0] // BLOCK):
            rows.append(jnp.sum(sq[i * BLOCK : (i + 1) * BLOCK].T, axis=0, keepdims=True))
    out_ref[...] = jnp.broadcast_to(jnp.concatenate(rows, axis=0)[None], out_ref.shape)


def lanes(head):
    return slice(head * HEAD, (head + 1) * HEAD)


class Pack:
    def __init__(self, heads, batch, blocks):
        self.heads, self.rows = heads, batch * blocks
        self.slot = 2 * LAYERS * heads
        self.step = self.slot + 1
        self.size = -(-(self.step + 1) // 8) * 8
        self.full = 2 * self.size + 2 * LAYERS * self.rows

    def gains(self, ref, layer, head):
        base = layer // LAYERS * self.size
        at = [base + (part * LAYERS + layer % LAYERS) * self.heads + head for part in range(2)]
        return [ref[i : i + 1, :] for i in at]

    def sums(self, layer):
        return slice(2 * self.size + layer * self.rows, 2 * self.size + (layer + 1) * self.rows)

    def second(self, ref, section=0):
        at = section * self.size + self.slot
        return ref[at : at + 1, :] > 0.5

    def late(self, ref, section=0):
        at = section * self.size + self.step
        return ref[at : at + 1, :] > 0.5


def first_kernel(x_ref, out_ref):
    batch, _, width = x_ref.shape
    found = []
    for b in range(batch):
        sq = 0.0
        for head in range(width // HEAD):
            xf = x_ref[b, :, lanes(head)].astype(jnp.float32)
            sq = sq + xf * xf
        found.append(sq)
    token_sums(found, out_ref)


def one_layer(pack, layer, x_refs, totals, pack_ref, y_ref):
    blocks = x_refs[0].shape[0] // BLOCK
    found = []
    for b, x_ref in enumerate(x_refs):
        scale = column(totals[b * blocks : (b + 1) * blocks])
        sq = 0.0
        for head in range(pack.heads):
            xf = x_ref[:, lanes(head)].astype(jnp.float32)
            y = head_layer(xf, scale, *pack.gains(pack_ref, layer, head))
            if y_ref is not None:
                y_ref[b, :, lanes(head)] = y
            yf = y.astype(jnp.float32)
            sq = sq + yf * yf
        found.append(sq)
    return found


def layer_kernel(pack, layer, outputs, x_ref, parts_ref, pack_ref, *refs):
    refs = list(refs)
    next_ref = refs.pop(0) if "pick" in outputs else None
    y_ref = refs.pop(0) if "y" in outputs else None
    pick_ref = refs.pop(0) if "pick" in outputs else None
    x_refs = [x_ref.at[b] for b in range(x_ref.shape[0])]
    found = one_layer(pack, layer, x_refs, jnp.sum(parts_ref[...], axis=0), pack_ref, y_ref)
    if pick_ref is not None:
        second = pack.second(next_ref)
        for head in range(pack.heads):
            pick_ref[:, lanes(head)] = either(second, y_ref[1, :, lanes(head)], y_ref[0, :, lanes(head)])
    token_sums(found, refs[-1])


def either(condition, there, here):
    return jnp.where(condition, there.astype(jnp.float32), here.astype(jnp.float32)).astype(jnp.bfloat16)


def choose_kernel(pack, y_ref, carry_ref, pack_ref, out_ref):
    second, late = pack.second(pack_ref), pack.late(pack_ref)
    for head in range(pack.heads):
        at = lanes(head)
        out_ref[:, at] = either(late, carry_ref[:, at], either(second, y_ref[1, :, at], y_ref[0, :, at]))


def pack_kernel(pack, own_ref, next_ref, *refs):
    *parts_refs, out_ref = refs
    out_ref[: pack.size, :] = own_ref[...]
    out_ref[pack.size : 2 * pack.size, :] = next_ref[...]
    for layer, parts_ref in enumerate(parts_refs):
        out_ref[pack.sums(layer), :] = jnp.sum(parts_ref[...], axis=0)


def repeat_kernel(pack, x0_ref, x1_ref, pack_ref, out_ref, a_ref, b_ref):
    refs = [(x0_ref, x1_ref), a_ref, b_ref, a_ref, out_ref]
    for layer in range(2 * LAYERS):
        x_refs = [refs[layer].at[b] for b in range(out_ref.shape[0])] if layer else refs[0]
        one_layer(pack, layer, x_refs, pack_ref[pack.sums(layer), :], pack_ref, refs[layer + 1])


def mirror_kernel(pack, x_ref, pack_ref, out_ref, y_ref):
    blocks = x_ref.shape[0] // BLOCK
    second, late = pack.second(pack_ref, 1), pack.late(pack_ref, 1)
    refs = [x_ref, y_ref, out_ref]
    for at in range(LAYERS):
        layer = LAYERS + at
        totals = pack_ref[pack.sums(layer), :]
        scale = column(jnp.where(second, totals[blocks : 2 * blocks], totals[:blocks]))
        for head in range(pack.heads):
            xf = refs[at][:, lanes(head)].astype(jnp.float32)
            y = head_layer(xf, scale, *pack.gains(pack_ref, layer, head))
            if at == LAYERS - 1:
                y = either(late, y, x_ref[:, lanes(head)])
            refs[at + 1][:, lanes(head)] = y


def exchange(parts):
    return lax.all_to_all(parts, "tensor", 0, 0, tiled=True)


def send(value, target):
    count = lax.axis_size("section")
    return lax.ppermute(value, "section", [(s, target(s) % count) for s in range(count)])


def around_x(hop):
    sections, members = lax.axis_size("section"), lax.axis_size("tensor")
    ys, count = members // X_LO, X_HI * X_LO
    layers_z = sections // (X_HI * CORES)

    def flat(z, x, core, y):
        x %= count
        return (((z % layers_z) * X_HI + x // X_LO) * CORES + core) * members + (x % X_LO) * ys + y

    pairs = []
    for z in range(layers_z):
        for x in range(count):
            for core in range(CORES):
                for y in range(ys):
                    middle = flat(z, x + 1, core, y)
                    pairs.append(
                        (middle, flat(z + x // X_LO, x + 2, core, y)) if hop else (flat(z, x, core, y), middle)
                    )
    return pairs


def after(value, *earlier):
    return lax.optimization_barrier((value, *earlier))[0]


def shards(held, norm_gain, key_gain, evict_slot, evict_step):
    x = held[0]
    batch, length, width = x.shape
    heads = width // HEAD
    pack = Pack(heads, batch, length // BLOCK)
    sections, members = lax.axis_size("section"), lax.axis_size("tensor")
    both, one = bf16(*x.shape), bf16(length, width)
    sums = f32(members, pack.rows, BLOCK)
    axes = ("section", "tensor")

    def layer(at, *outputs):
        shapes = {"y": both, "pick": one, "sums": sums}
        return call(functools.partial(layer_kernel, pack, at, outputs), tuple(shapes[name] for name in outputs), "layer", 400)

    facts = jnp.concatenate([evict_slot, evict_step]).astype(jnp.float32)
    own = jnp.concatenate(
        [
            norm_gain.reshape(-1, HEAD),
            key_gain.reshape(-1, HEAD),
            jnp.broadcast_to(facts[:, None], (2, HEAD)),
            jnp.zeros((pack.size - pack.step - 1, HEAD), jnp.float32),
        ],
        axis=0,
    )

    halfway = lax.ppermute(x[1], axes, around_x(0))
    found = call(first_kernel, sums, "first_sums")(x)
    moved0 = send(after(x[0], found), lambda s: s + 2)
    parts = [exchange(found)]
    y, found = layer(0, "y", "sums")(x, parts[0], own)
    moved1 = lax.ppermute(after(halfway, found), axes, around_x(1))
    ahead = send(after(own, found), lambda s: s - 1)
    parts.append(exchange(found))
    y, pick, found = layer(1, "y", "pick", "sums")(y, parts[1], own, ahead)
    carry = send(after(pick, found), lambda s: s + 1)
    parts.append(exchange(found))
    (found,) = layer(0, "sums")(y, parts[2], ahead)
    chosen = call(functools.partial(choose_kernel, pack), one, "choose")(y, after(carry, found), own)
    kept = send(chosen, lambda s: sections - 1 - s)
    parts.append(exchange(found))
    full = call(functools.partial(pack_kernel, pack), f32(pack.full, HEAD), "pack")(own, ahead, *parts)
    behind = send(full, lambda s: s + 2)
    mirrored = send(full, lambda s: sections - 2 - s)

    repeat = functools.partial(repeat_kernel, pack)
    final = call(repeat, both, "repeat", 1600, [both, both])(moved0, moved1, behind)
    stored = call(functools.partial(mirror_kernel, pack), one, "mirror", 400, [one])(kept, mirrored)
    return (final[None], stored[None])


def solution(mesh):
    return jax.shard_map(
        shards,
        mesh=mesh,
        in_specs=(
            P("section", None, None, "tensor"),
            P("section", None, "tensor"),
            P("section", None, "tensor"),
            P("section"),
            P("section"),
        ),
        out_specs=(P("section", None, None, "tensor"), P("section", None, "tensor")),
        check_vma=False,
    )
```

```python
import functools

import jax
import jax.numpy as jnp
from jax import lax
from jax.experimental import pallas as pl
from jax.experimental.pallas import tpu as pltpu
from jax.sharding import PartitionSpec as P

D = 12288
HEAD = 128
LAYERS = 2
BLOCK = 128
EPS = 1e-5
SCORE = 1.4426950408889634 / HEAD**0.5
X_LO = X_HI = CORES = 2

VMEM = pl.BlockSpec(memory_space=pltpu.VMEM)
PARAMS = pltpu.CompilerParams(vmem_limit_bytes=32 * 1024 * 1024)


def call(kernel, out_shape, name, mflop=1, scratch=()):
    several = isinstance(out_shape, tuple)

    def run(*operands):
        return pl.pallas_call(
            kernel,
            out_shape=out_shape,
            in_specs=[VMEM] * len(operands),
            out_specs=(VMEM,) * len(out_shape) if several else VMEM,
            scratch_shapes=[pltpu.VMEM(like.shape, like.dtype) for like in scratch],
            compiler_params=PARAMS,
            cost_estimate=pl.CostEstimate(
                flops=mflop * 1_000_000, bytes_accessed=1_000_000, transcendentals=mflop * 2_000
            ),
            name=name,
        )(*operands)

    return run


def f32(*shape):
    return jax.ShapeDtypeStruct(shape, jnp.float32)


def bf16(*shape):
    return jax.ShapeDtypeStruct(shape, jnp.bfloat16)


def column(total):
    inv = lax.rsqrt(total / D + EPS)
    rows = [jnp.broadcast_to(inv[i : i + 1], (BLOCK, BLOCK)).T for i in range(inv.shape[0])]
    return jnp.concatenate(rows, axis=0)


def head_layer(xf, scale, ngain, kgain):
    length = xf.shape[0]
    keep = lax.broadcasted_iota(jnp.int32, (BLOCK, BLOCK), 1) <= lax.broadcasted_iota(jnp.int32, (BLOCK, BLOCK), 0)
    h = xf * scale * ngain
    query = h.astype(jnp.bfloat16)
    keys = (h * (kgain * SCORE)).astype(jnp.bfloat16)
    values = jnp.concatenate([query, jnp.ones((length, HEAD), jnp.bfloat16)], axis=1)
    out = []
    for i in range(length // BLOCK):
        here = slice(i * BLOCK, (i + 1) * BLOCK)
        seen = (i + 1) * BLOCK
        s = lax.dot_general(
            query[here], keys[:seen], (((1,), (1,)), ((), ())), preferred_element_type=jnp.float32
        )
        last = jnp.where(keep, s[:, i * BLOCK :], jnp.float32(-1e30))
        s = last if i == 0 else jnp.concatenate([s[:, : i * BLOCK], last], axis=1)
        p = jnp.exp2(s - jnp.max(s, axis=1, keepdims=True)).astype(jnp.bfloat16)
        o = jnp.dot(p, values[:seen], preferred_element_type=jnp.float32)
        out.append((xf[here] + o[:, :HEAD] / o[:, HEAD:]).astype(jnp.bfloat16))
    return jnp.concatenate(out, axis=0)


def token_sums(squares, out_ref):
    rows = []
    for sq in squares:
        for i in range(sq.shape[0] // BLOCK):
            rows.append(jnp.sum(sq[i * BLOCK : (i + 1) * BLOCK].T, axis=0, keepdims=True))
    out_ref[...] = jnp.broadcast_to(jnp.concatenate(rows, axis=0)[None], out_ref.shape)


def lanes(head):
    return slice(head * HEAD, (head + 1) * HEAD)


class Pack:
    def __init__(self, heads, batch, blocks):
        self.heads, self.rows = heads, batch * blocks
        self.slot = 2 * LAYERS * heads
        self.step = self.slot + 1
        self.size = -(-(self.step + 1) // 8) * 8
        self.full = 2 * self.size + 2 * LAYERS * self.rows

    def gains(self, ref, layer, head):
        base = layer // LAYERS * self.size
        at = [base + (part * LAYERS + layer % LAYERS) * self.heads + head for part in range(2)]
        return [ref[i : i + 1, :] for i in at]

    def sums(self, layer):
        return slice(2 * self.size + layer * self.rows, 2 * self.size + (layer + 1) * self.rows)

    def second(self, ref, section=0):
        at = section * self.size + self.slot
        return ref[at : at + 1, :] > 0.5

    def late(self, ref, section=0):
        at = section * self.size + self.step
        return ref[at : at + 1, :] > 0.5


def first_kernel(x_ref, out_ref):
    batch, _, width = x_ref.shape
    found = []
    for b in range(batch):
        sq = 0.0
        for head in range(width // HEAD):
            xf = x_ref[b, :, lanes(head)].astype(jnp.float32)
            sq = sq + xf * xf
        found.append(sq)
    token_sums(found, out_ref)


def one_layer(pack, layer, x_refs, totals, pack_ref, y_ref):
    blocks = x_refs[0].shape[0] // BLOCK
    found = []
    for b, x_ref in enumerate(x_refs):
        scale = column(totals[b * blocks : (b + 1) * blocks])
        sq = 0.0
        for head in range(pack.heads):
            xf = x_ref[:, lanes(head)].astype(jnp.float32)
            y = head_layer(xf, scale, *pack.gains(pack_ref, layer, head))
            if y_ref is not None:
                y_ref[b, :, lanes(head)] = y
            yf = y.astype(jnp.float32)
            sq = sq + yf * yf
        found.append(sq)
    return found


def layer_kernel(pack, layer, outputs, x_ref, parts_ref, pack_ref, *refs):
    refs = list(refs)
    next_ref = refs.pop(0) if "pick" in outputs else None
    y_ref = refs.pop(0) if "y" in outputs else None
    pick_ref = refs.pop(0) if "pick" in outputs else None
    x_refs = [x_ref.at[b] for b in range(x_ref.shape[0])]
    found = one_layer(pack, layer, x_refs, jnp.sum(parts_ref[...], axis=0), pack_ref, y_ref)
    if pick_ref is not None:
        second = pack.second(next_ref)
        for head in range(pack.heads):
            pick_ref[:, lanes(head)] = either(second, y_ref[1, :, lanes(head)], y_ref[0, :, lanes(head)])
    token_sums(found, refs[-1])


def either(condition, there, here):
    return jnp.where(condition, there.astype(jnp.float32), here.astype(jnp.float32)).astype(jnp.bfloat16)


def choose_kernel(pack, y_ref, carry_ref, pack_ref, out_ref):
    second, late = pack.second(pack_ref), pack.late(pack_ref)
    for head in range(pack.heads):
        at = lanes(head)
        out_ref[:, at] = either(late, carry_ref[:, at], either(second, y_ref[1, :, at], y_ref[0, :, at]))


def pack_kernel(pack, own_ref, next_ref, *refs):
    *parts_refs, out_ref = refs
    out_ref[: pack.size, :] = own_ref[...]
    out_ref[pack.size : 2 * pack.size, :] = next_ref[...]
    for layer, parts_ref in enumerate(parts_refs):
        out_ref[pack.sums(layer), :] = jnp.sum(parts_ref[...], axis=0)


def repeat_kernel(pack, x0_ref, x1_ref, pack_ref, out_ref, a_ref, b_ref):
    refs = [(x0_ref, x1_ref), a_ref, b_ref, a_ref, out_ref]
    for layer in range(2 * LAYERS):
        x_refs = [refs[layer].at[b] for b in range(out_ref.shape[0])] if layer else refs[0]
        one_layer(pack, layer, x_refs, pack_ref[pack.sums(layer), :], pack_ref, refs[layer + 1])


def mirror_kernel(pack, x_ref, pack_ref, out_ref, y_ref):
    blocks = x_ref.shape[0] // BLOCK
    second, late = pack.second(pack_ref, 1), pack.late(pack_ref, 1)
    refs = [x_ref, y_ref, out_ref]
    for at in range(LAYERS):
        layer = LAYERS + at
        totals = pack_ref[pack.sums(layer), :]
        scale = column(jnp.where(second, totals[blocks : 2 * blocks], totals[:blocks]))
        for head in range(pack.heads):
            xf = refs[at][:, lanes(head)].astype(jnp.float32)
            y = head_layer(xf, scale, *pack.gains(pack_ref, layer, head))
            if at == LAYERS - 1:
                y = either(late, y, x_ref[:, lanes(head)])
            refs[at + 1][:, lanes(head)] = y


def exchange(parts):
    return lax.all_to_all(parts, "tensor", 0, 0, tiled=True)


def send(value, target):
    count = lax.axis_size("section")
    return lax.ppermute(value, "section", [(s, target(s) % count) for s in range(count)])


def around_x(hop):
    sections, members = lax.axis_size("section"), lax.axis_size("tensor")
    ys, count = members // X_LO, X_HI * X_LO
    layers_z = sections // (X_HI * CORES)

    def flat(z, x, core, y):
        x %= count
        return (((z % layers_z) * X_HI + x // X_LO) * CORES + core) * members + (x % X_LO) * ys + y

    pairs = []
    for z in range(layers_z):
        for x in range(count):
            for core in range(CORES):
                for y in range(ys):
                    middle = flat(z, x + 1, core, y)
                    pairs.append(
                        (middle, flat(z + x // X_LO, x + 2, core, y)) if hop else (flat(z, x, core, y), middle)
                    )
    return pairs


def after(value, *earlier):
    return lax.optimization_barrier((value, *earlier))[0]


def shards(held, norm_gain, key_gain, evict_slot, evict_step):
    x = held[0]
    batch, length, width = x.shape
    heads = width // HEAD
    pack = Pack(heads, batch, length // BLOCK)
    sections, members = lax.axis_size("section"), lax.axis_size("tensor")
    both, one = bf16(*x.shape), bf16(length, width)
    sums = f32(members, pack.rows, BLOCK)
    axes = ("section", "tensor")

    def layer(at, *outputs):
        shapes = {"y": both, "pick": one, "sums": sums}
        return call(functools.partial(layer_kernel, pack, at, outputs), tuple(shapes[name] for name in outputs), "layer", 400)

    facts = jnp.concatenate([evict_slot, evict_step]).astype(jnp.float32)
    own = jnp.concatenate(
        [
            norm_gain.reshape(-1, HEAD),
            key_gain.reshape(-1, HEAD),
            jnp.broadcast_to(facts[:, None], (2, HEAD)),
            jnp.zeros((pack.size - pack.step - 1, HEAD), jnp.float32),
        ],
        axis=0,
    )

    halfway = lax.ppermute(x[1], axes, around_x(0))
    found = call(first_kernel, sums, "first_sums")(x)
    moved0 = send(after(x[0], found), lambda s: s + 2)
    parts = [exchange(found)]
    y, found = layer(0, "y", "sums")(x, parts[0], own)
    moved1 = lax.ppermute(after(halfway, found), axes, around_x(1))
    ahead = send(after(own, found), lambda s: s - 1)
    parts.append(exchange(found))
    y = after(y, moved0, moved1)
    y, pick, found = layer(1, "y", "pick", "sums")(y, parts[1], own, ahead)
    carry = send(after(pick, found), lambda s: s + 1)
    parts.append(exchange(found))
    (found,) = layer(0, "sums")(y, parts[2], ahead)
    chosen = call(functools.partial(choose_kernel, pack), one, "choose")(y, after(carry, found), own)
    kept = send(chosen, lambda s: sections - 1 - s)
    parts.append(exchange(found))
    full = call(functools.partial(pack_kernel, pack), f32(pack.full, HEAD), "pack")(own, ahead, *parts)
    behind = send(full, lambda s: s + 2)
    mirrored = send(full, lambda s: sections - 2 - s)

    repeat = functools.partial(repeat_kernel, pack)
    final = call(repeat, both, "repeat", 1600, [both, both])(moved0, moved1, behind)
    stored = call(functools.partial(mirror_kernel, pack), one, "mirror", 400, [one])(kept, mirrored)
    return (final[None], stored[None])


def solution(mesh):
    return jax.shard_map(
        shards,
        mesh=mesh,
        in_specs=(
            P("section", None, None, "tensor"),
            P("section", None, "tensor"),
            P("section", None, "tensor"),
            P("section"),
            P("section"),
        ),
        out_specs=(P("section", None, None, "tensor"), P("section", None, "tensor")),
        check_vma=False,
    )
```
